512 devices in a mesh: band: 64 (over z, x, core), lev: 8 (over y).
Axes of the slice: x: 4, y: 8, z: 8, core: 2. Of those that a mesh axis runs over, the one named last changes fastest.
Arguments:
- control: bfloat16 [1280, 1280, 2, 128], P('band', 'lev'), may hold values from -6 to 6
- vertical_root: bfloat16 [1280, 128, 128], P('band'), may hold values from -0.5 to 0.5
- legendre: bfloat16 [1280, 32, 1280], P('band'), may hold values from -0.0034179688 to 0.0034179688
- wave_list: int32 [1280], replicated, may hold values from 0 to 1279, as said below
- row_length: int32 [32], replicated, may hold values from 2580 to 5136, as said below
Outputs:
- grid_field: float32 [64, 128, 5136], P('band', 'lev')
- grid_slope: float32 [64, 128, 5136], P('band', 'lev')
The draws below stay inside these ranges and needn't reach their ends.
Inputs may be any that keep to these rules, and one draw needn't show every extreme that they name: `wave_list`: every zonal wavenumber from 0 to 1279 appears once. The first 10 slots of each owner hold 10 consecutive wavenumbers in increasing order, starting at a multiple of 10 below 640; its last 10 slots hold 1279 minus those, in the same order. `row_length`: each entry is 20 + 4 i for a latitude row index i from 640 to 1279, and both ends occur.
All inputs are finite; a program needn't handle non-finite values.
Results may differ from the reference program's by a relative error of at most 0.0057.
Values may be sent and summed in bfloat16 or wider, within the bound.
A program may use at most 128 MiB of HBM per device.

```python
import math
import jax
import jax.numpy as jnp
from jax import lax

M = 1280
L = 128
OWN = 20
HALF = 10
NLATW = 64
NLATH = 32
LONMAX = 5136
LONBLK = 41


def draw_wave_list(key, part):
    key = jax.random.fold_in(key, 11)
    owners = M // OWN
    half_own = OWN // 2
    order = jax.random.permutation(key, owners).astype(jnp.int32)
    slots = jnp.arange(M, dtype=jnp.int32)
    within = slots % OWN
    lower = order[slots // OWN] * half_own + within
    return jnp.where(within < half_own, lower, M - 1 - (lower - half_own)).astype(jnp.int32)


def draw_row_length(key, part):
    key = jax.random.fold_in(key, 23)
    first_key, second_key = jax.random.split(key)
    indices = jax.random.randint(first_key, (NLATH,), M // 2, M).astype(jnp.int32)
    placed = jax.random.permutation(second_key, NLATH)
    indices = indices.at[placed[0]].set(M - 1)
    indices = indices.at[placed[1]].set(M // 2)
    return (20 + 4 * indices).astype(jnp.int32)


def shard_levels(own_key, shape, cuts, low, high):
    loudness, own = 1.0, jax.random.fold_in(own_key, 6)
    for position, parts in cuts:
        heights = jnp.exp(jax.random.uniform(jax.random.fold_in(own, position), (parts,), jnp.float32, low / len(cuts), high / len(cuts)))
        loudness = loudness * jnp.repeat(heights, shape[position] // parts).reshape([-1 if axis == position else 1 for axis in range(len(shape))])
    return loudness


def scatter_about(rng, shape, scale, reach, cuts=(), kind=jnp.bfloat16):
    values = jax.random.normal(rng, shape, jnp.float32) * scale
    if len(cuts) > 0:
        values = shard_levels(rng, shape, cuts, -0.22, 0.18) * values
    return jnp.clip(values, min=-reach, max=reach).astype(kind)


def setup_inputs(seed: int = 0) -> dict:
    arg_keys = jax.random.split(jax.random.key(seed), 6)
    control = scatter_about(arg_keys[0], (M, M, 2, L), 1.0, 6.0, ((0, 64), (1, 8)))
    vertical_root = scatter_about(arg_keys[1], (M, L, L), L ** -0.5, 0.5, ((0, 64),))
    legendre = scatter_about(arg_keys[2], (M, NLATH, M), (2 * M * M) ** -0.5, 0.0034179688, ((0, 64),))
    wave_list = draw_wave_list(jax.random.fold_in(arg_keys[5], 71), 0)
    row_length = draw_row_length(jax.random.fold_in(arg_keys[5], 71), 0)
    return {"control": control, "vertical_root": vertical_root, "legendre": legendre, "wave_list": wave_list, "row_length": row_length}


def row_degree(rows):
    block_pos = rows // OWN
    within = rows % OWN
    lower = block_pos * HALF + within
    return jnp.where(within < HALF, lower, M - 1 - (lower - HALF)).astype(jnp.int32)


def block_basis(wave_list, row_len):
    columns = jnp.arange(128, dtype=jnp.int32)
    phase_int = (wave_list[:, None] * columns[None, :]) % row_len
    angle_val = phase_int.astype(jnp.float32) * (2.0 * math.pi / row_len.astype(jnp.float32))
    weight_m = jnp.where(wave_list == 0, 1.0, 2.0).astype(jnp.float32)
    slope_m = weight_m * wave_list.astype(jnp.float32) / M
    cosine = jnp.cos(angle_val)
    sine_val = jnp.sin(angle_val)
    real_rows = jnp.concatenate([weight_m[:, None] * cosine, -slope_m[:, None] * sine_val], axis=1)
    imag_rows = jnp.concatenate([-weight_m[:, None] * sine_val, -slope_m[:, None] * cosine], axis=1)
    stacked = jnp.stack([real_rows, imag_rows], axis=1)
    return stacked.astype(jnp.bfloat16).reshape(2 * wave_list.shape[0], 256)


def twist_coeffs(coeffs, wave_list, row_len, starts):
    phase_int = (wave_list[None, :] * starts[:, None]) % row_len
    angle_val = phase_int.astype(jnp.float32) * (2.0 * math.pi / row_len.astype(jnp.float32))
    cosine = jnp.cos(angle_val)[:, :, None]
    sine_val = jnp.sin(angle_val)[:, :, None]
    real_part = coeffs[:, 0, :].astype(jnp.float32)[None]
    imag_part = coeffs[:, 1, :].astype(jnp.float32)[None]
    new_real = real_part * cosine - imag_part * sine_val
    new_imag = real_part * sine_val + imag_part * cosine
    twisted = jnp.stack([new_real, new_imag], axis=2).astype(jnp.bfloat16)
    return twisted.reshape(starts.shape[0], 2 * wave_list.shape[0], coeffs.shape[2])


def reference(control, vertical_root, legendre, wave_list, row_length):
    block_rows = 16

    def accumulate(partial_value, block_pos):
        northern, southern = partial_value
        first_row = block_pos * block_rows
        control_rows = lax.dynamic_slice_in_dim(control, first_row, block_rows, 0)
        vert_block = lax.dynamic_slice_in_dim(vertical_root, first_row, block_rows, 0)
        poly_block = lax.dynamic_slice_in_dim(legendre, first_row, block_rows, 2).astype(jnp.float32)
        degree = row_degree(first_row + jnp.arange(block_rows, dtype=jnp.int32))
        retained = degree[:, None] >= wave_list[None, :]
        masked = jnp.where(retained[:, :, None, None], control_rows, jnp.zeros((), jnp.bfloat16))
        correlated = jnp.einsum('nlk,nsck->nscl', vert_block.astype(jnp.float32), masked.astype(jnp.float32)).astype(jnp.bfloat16)
        corr_rows = correlated.astype(jnp.float32).reshape(block_rows, M, 2 * L)
        parity = jnp.where((degree[:, None] + wave_list[None, :]) % 2 == 0, 1.0, -1.0).astype(jnp.float32)
        northern = northern + jnp.einsum('shn,nsc->shc', poly_block, corr_rows)
        southern = southern + jnp.einsum('shn,nsc->shc', poly_block, corr_rows * parity[:, :, None])
        return (northern, southern), None

    zero_sums = jnp.zeros((M, NLATH, 2 * L), jnp.float32)
    (northern, southern), unused = lax.scan(accumulate, (zero_sums, zero_sums), jnp.arange(M // block_rows, dtype=jnp.int32))
    fourier = jnp.concatenate([northern, southern[:, ::-1]], axis=1).astype(jnp.bfloat16).reshape(M, NLATW, 2, L)

    def per_row(lat_pos):
        mirror_pos = jnp.where(lat_pos < NLATH, lat_pos, NLATW - 1 - lat_pos)
        row_len = row_length[mirror_pos]
        coeffs = lax.dynamic_index_in_dim(fourier, lat_pos, 1, keepdims=False)
        starts = 128 * jnp.arange(LONBLK, dtype=jnp.int32)
        twisted = twist_coeffs(coeffs, wave_list, row_len, starts)
        basis_block = block_basis(wave_list, row_len)
        products = jnp.einsum('bkl,kt->lbt', twisted.astype(jnp.float32), basis_block.astype(jnp.float32))
        field_row = products[:, :, :128].reshape(L, LONBLK * 128)[:, :LONMAX]
        slope_row = products[:, :, 128:].reshape(L, LONBLK * 128)[:, :LONMAX]
        inside = (jnp.arange(LONMAX, dtype=jnp.int32) < row_len)[None, :]
        zero_val = jnp.zeros((), jnp.float32)
        return jnp.where(inside, field_row, zero_val), jnp.where(inside, slope_row, zero_val)

    grid_field, grid_slope = lax.map(per_row, jnp.arange(NLATW, dtype=jnp.int32))
    return grid_field, grid_slope
```

```python
import functools

import jax
import jax.numpy as jnp
from jax import lax
from jax.experimental import pallas as pl
from jax.experimental.pallas import tpu as pltpu
from jax.sharding import PartitionSpec as P

M = 1280
LONMAX = 5136
BLOCKS = 41
F32 = jnp.float32
BF16 = jnp.bfloat16
MESH = pl.DeviceIdType.MESH

SIN_TERMS = (3.14159264, -5.16771008, 2.55007752, -0.598291286, 0.0776576603)
COS_TERMS = (0.999999953, -4.93479283, 4.05841135, -1.33187657, 0.219689611)


def iota(shape, dim):
    return lax.broadcasted_iota(jnp.int32, shape, dim)


def dot_nt(a, b):
    return lax.dot_general(a, b, (((1,), (1,)), ((), ())), preferred_element_type=F32)


def dot_nn(a, b):
    return lax.dot_general(a, b, (((1,), (0,)), ((), ())), preferred_element_type=F32)


def polynomial(terms, square):
    total = jnp.full_like(square, terms[-1])
    for term in terms[-2::-1]:
        total = total * square + term
    return total


def turn(product, row_len, inverse):
    doubled = product * 2.0
    halves = jnp.floor(doubled * inverse + 0.5)
    part = (doubled - halves * row_len) * inverse
    even = halves * 0.5
    sign = 1.0 - 4.0 * (even - jnp.floor(even))
    square = part * part
    return polynomial(COS_TERMS, square) * sign, polynomial(SIN_TERMS, square) * part * sign


def exchange(x):
    row, lane = iota((8, 128), 0), iota((8, 128), 1)
    for step in (4, 2, 1):
        row_bit = (row & step) != 0
        lane_bit = (lane & (16 * step)) != 0
        if step == 4:
            moved = pltpu.roll(pltpu.roll(x, 4, 0), 64, 1)
        else:
            up = pltpu.roll(pltpu.roll(x, step, 0), 128 - 16 * step, 1)
            down = pltpu.roll(pltpu.roll(x, 8 - step, 0), 16 * step, 1)
            moved = jnp.where(row_bit, up, down)
        x = jnp.where(row_bit == lane_bit, x, moved)
    return x


def kernel(
    ctrl_hbm, vert_hbm, leg_hbm, waves, rows_len,
    out_f, out_s,
    ctrl, vert, leg, prod, stage, send1, recv1, w0, w1, w2, w3, send2, recv2, cos_t, sin_t, basis, tw,
    in_sem, ssem1, rsem1, ssem2, rsem2,
):
    band, lev = lax.axis_index("band"), lax.axis_index("lev")
    z, rc = lax.div(band, 8), lax.rem(band, 8)
    xpos, core = lax.div(rc, 2), lax.rem(rc, 2)
    own_line = z == lev

    barrier = pltpu.get_barrier_semaphore()

    def greet(e, carry):
        @pl.when(jnp.logical_not(jnp.logical_and(e == band, own_line)))
        def _():
            pl.semaphore_signal(barrier, inc=1, device_id=(e, z), device_id_type=MESH)

        @pl.when(e != band)
        def _():
            pl.semaphore_signal(barrier, inc=1, device_id=(e, lev), device_id_type=MESH)

        return carry

    lax.fori_loop(0, 64, greet, 0)
    copies = [
        pltpu.make_async_copy(src, dst, in_sem.at[n])
        for n, (src, dst) in enumerate(((ctrl_hbm, ctrl), (vert_hbm, vert), (leg_hbm, leg)))
    ]
    for copy in copies:
        copy.start()
    stage[...] = jnp.zeros_like(stage)
    copies[0].wait()
    copies[1].wait()

    def products(q, carry):
        for h in range(2):
            n = q + 10 * h
            prod[n] = dot_nt(ctrl[n], vert[n])
        return carry

    lax.fori_loop(0, 10, products, 0)
    pl.semaphore_wait(barrier, jnp.where(own_line, 126, 127))

    row24 = iota((24, 128), 0)
    place24 = lax.shift_right_arithmetic(row24 - 4, 1)
    body24 = row24 >= 4

    def owner_step(d, carry):
        owner = lax.rem(xpos + lax.div(d, 2), 4) * 2 + lax.rem(core + d, 2)
        base = waves[(lev * 8 + owner) * 20]
        first = pl.multiple_of(owner * 40, 8)

        def degree_step(k, diag):
            high = prod[10 + k, pl.ds(first, 40), :]
            low = pltpu.roll(prod[k, pl.ds(first, 24), :], 4, 0)
            reach = 10 * band + k - base
            top = high[16:]
            mid = jnp.where(jnp.logical_and(body24, place24 <= reach), low, top)
            diag = jnp.where(jnp.logical_and(body24, place24 == reach), top, diag)
            parts = (high[:8], high[8:16], mid[:8], mid[8:16], mid[16:])
            places = (k, 16 + k, jnp.where(k < 6, 10 + k, 20 + k), 32 + k, 48 + k)
            for part, place in zip(parts, places):
                stage[pl.ds(place, 8, stride=64), :] = exchange(part)
            return diag

        diag = lax.fori_loop(0, 10, degree_step, jnp.zeros((24, 128), F32))
        for n, place in enumerate((30, 42, 58)):
            stage[pl.ds(place, 8, stride=64), :] = exchange(diag[8 * n : 8 * n + 8])
        for y in range(8):
            send1[d, y] = stage[64 * y : 64 * y + 64, :].astype(BF16)

        def send_step(e, inner):
            y = lax.rem(e + z + d, 8)
            mine = jnp.logical_and(jnp.logical_and(own_line, y == lev), owner == rc)

            @pl.when(jnp.logical_not(mine))
            def _():
                pltpu.make_async_remote_copy(
                    src_ref=send1.at[d, y], dst_ref=recv1.at[band], send_sem=ssem1, recv_sem=rsem1,
                    device_id=(lev * 8 + owner, y), device_id_type=MESH,
                ).start()

            @pl.when(mine)
            def _():
                pltpu.make_async_copy(send1.at[d, y], recv1.at[band], rsem1).start()

            return inner

        lax.fori_loop(0, 8, send_step, 0)
        return carry

    lax.fori_loop(0, 8, owner_step, 0)

    copies[2].wait()
    own_base = waves[band * 20]
    lane = iota((32, 128), 1)
    slot = lane & 15
    alt = (1 - 2 * (lane & 1)).astype(F32)
    diag_lane = slot == 10
    zero = jnp.zeros((32, 128), F32)
    late = slot >= 10
    late5 = jnp.logical_and(late, slot <= 14)

    def weigh(bb, carry):
        start = pl.multiple_of(lax.div(bb * 5, 4) * 128, 128)
        cols = pl.ds(pl.multiple_of(bb * 128, 128), 128)
        pick_row, pick_lane = iota((256, 128), 0), iota((256, 128), 1)
        pick_slot = pick_lane & 15
        target = 32 * lax.rem(bb, 4) + 20 * lax.shift_right_logical(pick_lane, 4) + pick_slot
        valid = pick_slot < 10
        pick_low = jnp.where(jnp.logical_and(valid, pick_row == target), 1.0, 0.0).astype(BF16)
        pick_high = jnp.where(jnp.logical_and(valid, pick_row == target + 10), 1.0, 0.0).astype(BF16)
        high = dot_nn(leg[:, pl.ds(start, 256)], pick_high)
        low = dot_nn(leg[:320, pl.ds(start, 256)], pick_low)
        degree = 10 * (8 * bb + lax.shift_right_logical(lane, 4)) + slot

        def put(group, place, parts):
            for n, part in enumerate(parts):
                at = pl.ds(place + 32 * n, 32)
                if group == 2:
                    w0[at, cols] = jnp.where(late, pltpu.roll(part, 10, 1), zero).astype(BF16)
                    w1[at, cols] = jnp.where(late5, pltpu.roll(part, 4, 1), zero).astype(BF16)
                else:
                    (w0, w1, None, w2, w3)[group][at, cols] = part.astype(BF16)

        for i in range(10):
            sign = 1.0 - 2.0 * (i % 2)
            part = high[32 * i : 32 * i + 32]
            place = (i % 4) * 64 if i < 8 else 256 + (i - 8) * 64
            put(i // 4, place, (part, part * (alt * -sign)))
        for i in range(10):
            sign = 1.0 - 2.0 * (i % 2)
            first = jnp.where(degree >= own_base + i, low[32 * i : 32 * i + 32], zero)
            part = high[320 + 32 * i : 352 + 32 * i]
            second = jnp.where(degree < own_base + i, part, zero)
            second = jnp.where(diag_lane, pltpu.roll(part, 10 - i, 1), second)
            signs = alt * sign
            place = 384 + i * 128 if i < 2 else ((i - 2) % 4) * 128
            put(
                (i + 2) // 4 + 2, place,
                (first, first * signs, second, second * jnp.where(diag_lane, 1.0, signs)),
            )
        return carry

    lax.fori_loop(0, 8, weigh, 0)

    row_len = rows_len[jnp.where(band < 32, band, 63 - band)].astype(F32)
    inverse = 1.0 / jnp.full((1, 128), row_len, F32)
    one_lane = iota((1, 128), 1)

    def gather_base(o, found):
        return jnp.where((one_lane & 63) == o, waves[o * 20], found)

    bases = lax.fori_loop(0, 64, gather_base, jnp.zeros((1, 128), jnp.int32))
    half = lax.shift_right_logical(one_lane, 6)

    def tables(tile, carry):
        fine = lax.rem(tile, 4)
        pair = lax.div(tile, 4)
        slots = jnp.where(pair == 2, 16 + 2 * fine + half, 8 * pair + 4 * half + fine)
        wave = jnp.where(slots < 10, bases + slots, M - 1 - bases - (slots - 10)).astype(F32)
        cols = pl.ds(pl.multiple_of(tile * 128, 128), 128)
        starts = iota((48, 128), 0).astype(F32) * 128.0
        cosine, sine = turn(starts * wave, row_len, inverse)
        cos_t[:, cols] = cosine
        sin_t[:, cols] = sine
        columns = iota((128, 128), 0).astype(F32)
        cosine, sine = turn(columns * wave, row_len, inverse)
        weight = jnp.where(wave == 0.0, 1.0, 2.0)
        slope = weight * wave * (1.0 / M)
        real = pl.ds(pl.multiple_of(tile * 128, 128), 128)
        imag = pl.ds(pl.multiple_of(1280 + tile * 128, 128), 128)
        basis[real, :128] = (cosine * weight).T.astype(BF16)
        basis[imag, :128] = (sine * -weight).T.astype(BF16)
        basis[real, 128:] = (sine * -slope).T.astype(BF16)
        basis[imag, 128:] = (cosine * -slope).T.astype(BF16)
        return carry

    lax.fori_loop(0, 10, tables, 0)

    pltpu.make_async_copy(recv1, recv1, rsem1).wait()
    wide = iota((64, 128), 1)
    chunk = lax.shift_right_logical(wide, 5)

    def rows16(n):
        return recv1[:, 16 * n : 16 * n + 16, :].reshape(1024, 128)

    def diagonal(value, start, step, where_chunks):
        total = None
        for n, at in enumerate(where_chunks):
            piece = value[start + step * n : start + step * n + 64]
            total = piece if total is None else jnp.where(chunk == at, piece, total)
        return total

    out0 = dot_nn(w0[...], rows16(0))
    out1 = dot_nn(w1[...], rows16(1))
    out2 = dot_nn(w2[...], rows16(2))
    out3 = dot_nn(w3[...], rows16(3))
    mixed = out0[256:] + out1[256:]
    every = (0, 1, 2, 3)
    lower = wide < 64
    back2 = pltpu.roll(diagonal(mixed, 128, 128, (2, 3)), 64, 1)
    back3 = pltpu.roll(diagonal(out2, 0, 128, every), 64, 1)
    back4 = pltpu.roll(diagonal(out3, 0, 128, every), 64, 1)
    groups = (
        diagonal(out0, 0, 64, every) + jnp.where(lower, back2, back3),
        diagonal(out1, 0, 64, every) + jnp.where(lower, back3, back4),
        jnp.where(lower, diagonal(mixed, 0, 64, (0, 1)) + back4, diagonal(mixed, 192, 128, (2, 3))),
        diagonal(out2, 64, 128, every),
        diagonal(out3, 64, 128, every),
    )
    for n, group in enumerate(groups):
        send2[pl.ds(n, 64, stride=8), :] = group

    def fourier_step(e, carry):
        lat = lax.rem(z + e, 8) * 8 + (rc ^ lax.div(e, 8))
        row = pl.multiple_of(jnp.where(lat < 32, lat, 95 - lat) * 8, 8)
        src, dst = send2.at[pl.ds(row, 8), :], recv2.at[pl.ds(pl.multiple_of(band * 8, 8), 8), :]

        @pl.when(lat != band)
        def _():
            pltpu.make_async_remote_copy(
                src_ref=src, dst_ref=dst, send_sem=ssem2, recv_sem=rsem2, device_id=(lat, lev), device_id_type=MESH
            ).start()

        @pl.when(lat == band)
        def _():
            pltpu.make_async_copy(src, dst, rsem2).start()

        return carry

    lax.fori_loop(0, 64, fourier_step, 0)
    pltpu.make_async_copy(recv2, recv2, rsem2).wait()

    def received(n):
        return recv2[pl.ds(n, 64, stride=8), :].astype(BF16).astype(F32)

    first_two = jnp.concatenate([received(0), received(1)], axis=0).T
    second_two = jnp.concatenate([received(2), received(3)], axis=0).T
    last_one = received(4)
    last_one = jnp.concatenate([last_one, last_one], axis=0).T
    left = iota((16, 128), 1) < 64

    def coefficients(part):
        tiles = []
        for source in (first_two, second_two):
            for fine in range(4):
                at = fine * 32 + part * 16
                tiles.append(source[at : at + 16])
        for fine in (0, 2):
            at = fine * 32 + part * 16
            tiles.append(jnp.where(left, last_one[at : at + 16], last_one[at + 32 : at + 48]))
        return tiles

    reals, imags = coefficients(0), coefficients(1)

    def twist(start, count):
        for tile in range(10):
            cols = slice(tile * 128, tile * 128 + 128)
            imag_cols = slice(1280 + tile * 128, 1408 + tile * 128)
            cosines, sines = cos_t[pl.ds(start, 8), cols], sin_t[pl.ds(start, 8), cols]
            real, imag = reals[tile], imags[tile]
            for n in range(count):
                at = pl.ds(pl.multiple_of((start + n) * 16, 16), 16)
                cosine, sine = cosines[n : n + 1], sines[n : n + 1]
                tw[at, cols] = (real * cosine - imag * sine).astype(BF16)
                tw[at, imag_cols] = (real * sine + imag * cosine).astype(BF16)

    def twist_step(n, carry):
        twist(pl.multiple_of(n * 8, 8), 8)
        return carry

    lax.fori_loop(0, 5, twist_step, 0)
    twist(40, 1)

    result = dot_nn(tw[...], basis[...])
    for b in range(BLOCKS):
        inside = (iota((16, 128), 1) + 128 * b).astype(F32) < row_len
        width = min(128, LONMAX - 128 * b)
        for out, at in ((out_f, 0), (out_s, 128)):
            piece = jnp.where(inside, result[16 * b : 16 * b + 16, at : at + 128], 0.0)
            out[0, :, 128 * b : 128 * b + width] = piece[:, :width]

    @pl.when(own_line)
    def _():
        pltpu.make_async_copy(send1_flat(send1), send1_flat(send1), ssem1).wait()

    @pl.when(jnp.logical_not(own_line))
    def _():
        pltpu.make_async_copy(send1, send1, ssem1).wait()

    pltpu.make_async_copy(send2.at[pl.ds(0, 504), :], send2.at[pl.ds(0, 504), :], ssem2).wait()


def send1_flat(send1):
    return send1.reshape(64, 64, 128).at[pl.ds(0, 63)]


def shards(control, vertical_root, legendre, wave_list, row_length):
    shape = jax.ShapeDtypeStruct((1, 16, LONMAX), F32)
    vmem, smem, hbm = (
        pl.BlockSpec(memory_space=pltpu.VMEM),
        pl.BlockSpec(memory_space=pltpu.SMEM),
        pl.BlockSpec(memory_space=pl.ANY),
    )
    return pl.pallas_call(
        kernel,
        out_shape=(shape, shape),
        in_specs=[hbm, hbm, hbm, smem, smem],
        out_specs=(vmem, vmem),
        scratch_shapes=[
            pltpu.VMEM((20, 320, 128), BF16),
            pltpu.VMEM((20, 128, 128), BF16),
            pltpu.VMEM((640, 1280), BF16),
            pltpu.VMEM((20, 320, 128), F32),
            pltpu.VMEM((512, 128), F32),
            pltpu.VMEM((8, 8, 64, 128), BF16),
            pltpu.VMEM((64, 64, 128), BF16),
            pltpu.VMEM((640, 1024), BF16),
            pltpu.VMEM((640, 1024), BF16),
            pltpu.VMEM((512, 1024), BF16),
            pltpu.VMEM((512, 1024), BF16),
            pltpu.VMEM((512, 128), F32),
            pltpu.VMEM((512, 128), F32),
            pltpu.VMEM((48, 1280), F32),
            pltpu.VMEM((48, 1280), F32),
            pltpu.VMEM((2560, 256), BF16),
            pltpu.VMEM((656, 2560), BF16),
            pltpu.SemaphoreType.DMA((3,)),
            pltpu.SemaphoreType.DMA,
            pltpu.SemaphoreType.DMA,
            pltpu.SemaphoreType.DMA,
            pltpu.SemaphoreType.DMA,
        ],
        compiler_params=pltpu.CompilerParams(
            collective_id=0, has_side_effects=True, vmem_limit_bytes=56 * 2**20
        ),
    )(
        control.reshape(20, 320, 128),
        vertical_root,
        legendre.reshape(640, 1280),
        wave_list,
        row_length,
    )


def solution(mesh):
    placed = (P("band", "lev", None, None), P("band", None, None), P("band", None, None), P(), P())
    return jax.shard_map(
        shards,
        mesh=mesh,
        in_specs=placed,
        out_specs=(P("band", "lev", None), P("band", "lev", None)),
        check_vma=False,
    )
```

```python
import functools

import jax
import jax.numpy as jnp
from jax import lax
from jax.experimental import pallas as pl
from jax.experimental.pallas import tpu as pltpu
from jax.sharding import PartitionSpec as P

M = 1280
LONMAX = 5136
BLOCKS = 41
F32 = jnp.float32
BF16 = jnp.bfloat16
MESH = pl.DeviceIdType.MESH

SIN_TERMS = (3.14159264, -5.16771008, 2.55007752, -0.598291286, 0.0776576603)
COS_TERMS = (0.999999953, -4.93479283, 4.05841135, -1.33187657, 0.219689611)


def iota(shape, dim):
    return lax.broadcasted_iota(jnp.int32, shape, dim)


def dot_nt(a, b):
    return lax.dot_general(a, b, (((1,), (1,)), ((), ())), preferred_element_type=F32)


def dot_nn(a, b):
    return lax.dot_general(a, b, (((1,), (0,)), ((), ())), preferred_element_type=F32)


def polynomial(terms, square):
    total = jnp.full_like(square, terms[-1])
    for term in terms[-2::-1]:
        total = total * square + term
    return total


def turn(product, row_len, inverse):
    doubled = product * 2.0
    halves = jnp.floor(doubled * inverse + 0.5)
    part = (doubled - halves * row_len) * inverse
    even = halves * 0.5
    sign = 1.0 - 4.0 * (even - jnp.floor(even))
    square = part * part
    return polynomial(COS_TERMS, square) * sign, polynomial(SIN_TERMS, square) * part * sign


def exchange(rows):
    group = lax.shift_right_logical(iota((8, 128), 1), 4)
    turned = [pltpu.roll(row, 16 * r, 1) if r else row for r, row in enumerate(rows)]
    for step in (1, 2, 4):
        odd = (group & step) != 0
        turned = [jnp.where(odd, turned[(n + step) % 8], turned[n]) for n in range(8)]
    found = [turned[(8 - y) % 8] for y in range(8)]
    return [pltpu.roll(row, 128 - 16 * y, 1) if y else row for y, row in enumerate(found)]


def kernel(
    ctrl_hbm, vert_hbm, leg_hbm, waves_hbm, rows_hbm,
    out_f, out_s,
    ctrl, vert, waves, leg, rows_len, prod, send1, recv1, w0, w1, w2, w3, send2, recv2, cos_t, sin_t, basis, tw,
    in_sem, ssem1, rsem1, ssem2, rsem2,
):
    band, lev = lax.axis_index("band"), lax.axis_index("lev")
    z, rc = lax.div(band, 8), lax.rem(band, 8)
    xpos, core = lax.div(rc, 2), lax.rem(rc, 2)
    own_line = z == lev

    sources = (ctrl_hbm, vert_hbm, waves_hbm, leg_hbm, rows_hbm)
    copies = [
        pltpu.make_async_copy(src, dst, in_sem.at[n])
        for n, (src, dst) in enumerate(zip(sources, (ctrl, vert, waves, leg, rows_len)))
    ]
    for copy in copies:
        copy.start()

    barrier = pltpu.get_barrier_semaphore()

    def greet(e, carry):
        @pl.when(jnp.logical_not(jnp.logical_and(e == band, own_line)))
        def _():
            pl.semaphore_signal(barrier, inc=1, device_id=(e, z), device_id_type=MESH)

        @pl.when(e != band)
        def _():
            pl.semaphore_signal(barrier, inc=1, device_id=(e, lev), device_id_type=MESH)

        return carry

    lax.fori_loop(0, 64, greet, 0)
    copies[0].wait()
    copies[1].wait()

    def products(q, carry):
        for n in range(5):
            half = lax.div(q, 2)
            degree = 5 * q + n
            at = pl.multiple_of((degree + 6 * half) * 320, 8)
            prod[pl.ds(at, 320), :] = dot_nt(ctrl[degree], vert[degree])
        return carry

    lax.fori_loop(0, 4, products, 0)
    copies[2].wait()
    pl.semaphore_wait(barrier, jnp.where(own_line, 126, 127))

    sub = iota((8, 128), 0)

    def owner_step(d, carry):
        owner = lax.rem(xpos + lax.div(d, 2), 4) * 2 + lax.rem(core + d, 2)
        base = waves[(lev * 8 + owner) * 20]
        first = owner * 40
        shift = 10 * band - base
        on_diagonal = shift == 0

        def load(half, k, row):
            return prod[pl.ds(first + ((16 * half + k) * 320 + row), 8, stride=320), :]

        def degrees(row, k):
            high = load(1, k, row)
            if row < 20:
                return high
            return jnp.where(sub + (k + shift) >= (row - 20) // 2, load(0, k, row - 20), high)

        def diagonal_row(row, place):
            if row < 20:
                return jnp.zeros((8, 128), F32)
            return jnp.where(on_diagonal, load(1, (row - 20) // 2 - place, row), 0.0)

        def extra_a(r):
            rows = jnp.where(sub < 6, diagonal_row(24 + r, 5), degrees(r, 2))
            rows = jnp.where(sub < 5, degrees(24 + r, 5), rows)
            rows = jnp.where(sub < 3, diagonal_row(32 + r, 2), rows)
            return jnp.where(sub < 2, degrees(32 + r, 8), rows)

        def extra_b(r):
            rows = jnp.where(sub < 5, degrees(8 + r, 5), 0.0)
            rows = jnp.where(sub < 3, diagonal_row(16 + r, 2), rows)
            return jnp.where(sub < 2, degrees(16 + r, 8), rows)

        def main(group):
            return exchange([degrees(8 * group + r, 0) for r in range(8)])

        for tile in range(3):
            top = main(2 * tile)
            low = main(2 * tile + 1) if tile < 2 else exchange([extra_a(r) for r in range(8)])
            for y in range(8):
                send1[8 * d + y, 16 * tile : 16 * tile + 16, :] = jnp.concatenate([top[y], low[y]], axis=0).astype(BF16)
        low = exchange([extra_b(r) for r in range(8)])
        for y in range(8):
            send1[8 * d + y, 48:56, :] = low[y].astype(BF16)

        def send_step(e, inner):
            y = lax.rem(e + z + d, 8)
            mine = jnp.logical_and(jnp.logical_and(own_line, y == lev), owner == rc)

            @pl.when(jnp.logical_not(mine))
            def _():
                pltpu.make_async_remote_copy(
                    src_ref=send1.at[8 * d + y], dst_ref=recv1.at[band], send_sem=ssem1, recv_sem=rsem1,
                    device_id=(lev * 8 + owner, y), device_id_type=MESH,
                ).start()

            @pl.when(mine)
            def _():
                pltpu.make_async_copy(send1.at[8 * d + y], recv1.at[band], rsem1).start()

            return inner

        lax.fori_loop(0, 8, send_step, 0)
        return carry

    lax.fori_loop(0, 8, owner_step, 0)

    copies[3].wait()
    copies[4].wait()
    own_base = waves[band * 20]
    lane = iota((32, 128), 1)
    slot = lane & 15
    alt = (1 - 2 * (lane & 1)).astype(F32)
    diag_lane = slot == 10
    zero = jnp.zeros((32, 128), F32)
    early8 = slot < 8

    def moved(part, by, low, high):
        return jnp.where(jnp.logical_and(slot >= low, slot <= high), pltpu.roll(part, by % 128, 1), zero)

    def weigh(bb, carry):
        start = pl.multiple_of(lax.div(bb * 5, 4) * 128, 128)
        cols = pl.ds(pl.multiple_of(bb * 128, 128), 128)
        pick_row, pick_lane = iota((256, 128), 0), iota((256, 128), 1)
        pick_slot = pick_lane & 15
        target = 32 * lax.rem(bb, 4) + 20 * lax.shift_right_logical(pick_lane, 4) + pick_slot
        valid = pick_slot < 10
        pick_low = jnp.where(jnp.logical_and(valid, pick_row == target), 1.0, 0.0).astype(BF16)
        pick_high = jnp.where(jnp.logical_and(valid, pick_row == target + 10), 1.0, 0.0).astype(BF16)
        high = dot_nn(leg[:, pl.ds(start, 256)], pick_high)
        low = dot_nn(leg[:320, pl.ds(start, 256)], pick_low)
        degree = 10 * (8 * bb + lax.shift_right_logical(lane, 4)) + slot

        def put(group, place, parts):
            for n, part in enumerate(parts):
                first8 = jnp.where(early8, part, zero)
                targets = (
                    ((w0, 0, first8), (w2, 1024, moved(part, 6, 14, 15))),
                    ((w0, 256, moved(part, 8, 8, 15)), (w3, 384, moved(part, -5, 3, 4))),
                    ((w1, 0, first8), (w3, 0, moved(part, -8, 0, 2))),
                    ((w1, 384, moved(part, 8, 8, 15)), (w2, 512, moved(part, 3, 11, 13))),
                    ((w2, 0, part),),
                )[group]
                for ref, start, value in targets:
                    ref[pl.ds(start + place + 32 * n, 32), cols] = value.astype(BF16)

        for i in range(10):
            sign = 1.0 - 2.0 * (i % 2)
            part = high[32 * i : 32 * i + 32]
            place = (i % 4) * 64
            put(i // 4, place, (part, part * (alt * -sign)))
        for i in range(10):
            sign = 1.0 - 2.0 * (i % 2)
            first = jnp.where(degree >= own_base + i, low[32 * i : 32 * i + 32], zero)
            part = high[320 + 32 * i : 352 + 32 * i]
            second = jnp.where(degree < own_base + i, part, zero)
            second = jnp.where(diag_lane, pltpu.roll(part, 10 - i, 1), second)
            signs = alt * sign
            place = 128 + i * 128 if i < 2 else ((i - 2) % 4) * 128
            put(
                (i + 2) // 4 + 2, place,
                (first, first * signs, second, second * jnp.where(diag_lane, 1.0, signs)),
            )
        return carry

    lax.fori_loop(0, 8, weigh, 0)

    row_len = rows_len[jnp.where(band < 32, band, 63 - band)].astype(F32)
    inverse = 1.0 / jnp.full((1, 128), row_len, F32)
    one_lane = iota((1, 128), 1)

    def gather_base(o, found):
        return jnp.where((one_lane & 63) == o, waves[o * 20], found)

    bases = lax.fori_loop(0, 64, gather_base, jnp.zeros((1, 128), jnp.int32))
    half = lax.shift_right_logical(one_lane, 6)

    def tables(tile, carry):
        fine = lax.rem(tile, 4)
        pair = lax.div(tile, 4)
        slots = jnp.where(pair == 2, 16 + 2 * fine + half, 8 * pair + 4 * half + fine)
        wave = jnp.where(slots < 10, bases + slots, M - 1 - bases - (slots - 10)).astype(F32)
        cols = pl.ds(pl.multiple_of(tile * 128, 128), 128)
        starts = iota((48, 128), 0).astype(F32) * 128.0
        cosine, sine = turn(starts * wave, row_len, inverse)
        cos_t[:, cols] = cosine
        sin_t[:, cols] = sine
        columns = iota((128, 128), 0).astype(F32)
        cosine, sine = turn(columns * wave, row_len, inverse)
        weight = jnp.where(wave == 0.0, 1.0, 2.0)
        slope = weight * wave * (1.0 / M)
        real = pl.ds(pl.multiple_of(tile * 128, 128), 128)
        imag = pl.ds(pl.multiple_of(1280 + tile * 128, 128), 128)
        basis[real, :128] = (cosine * weight).T.astype(BF16)
        basis[imag, :128] = (sine * -weight).T.astype(BF16)
        basis[real, 128:] = (sine * -slope).T.astype(BF16)
        basis[imag, 128:] = (cosine * -slope).T.astype(BF16)
        return carry

    lax.fori_loop(0, 10, tables, 0)

    pltpu.make_async_copy(recv1, recv1, rsem1).wait()
    wide = iota((64, 128), 1)
    chunk = lax.shift_right_logical(wide, 5)

    def rows16(n):
        if n < 3:
            return recv1[:, 16 * n : 16 * n + 16, :].reshape(1024, 128)
        rest = recv1[:, 48:56, :]
        return jnp.concatenate([rest, jnp.zeros_like(rest)], axis=1).reshape(1024, 128)

    def diagonal(value, start, step, where_chunks):
        total = None
        for n, at in enumerate(where_chunks):
            piece = value[start + step * n : start + step * n + 64]
            total = piece if total is None else jnp.where(chunk == at, piece, total)
        return total

    out0 = dot_nn(w0[...], rows16(0))
    out1 = dot_nn(w1[...], rows16(1))
    out2 = dot_nn(w2[...], rows16(2))
    out3 = dot_nn(w3[...], rows16(3))
    sum0 = out0[:256] + out2[1024:]
    sum1 = out0[256:] + out3[384:]
    sum2 = out1[:384] + out3[:384]
    sum3 = out1[384:] + out2[512:1024]
    sum4 = out2[:512]
    every = (0, 1, 2, 3)
    lower = wide < 64
    back2 = pltpu.roll(diagonal(sum2, 128, 128, (2, 3)), 64, 1)
    back3 = pltpu.roll(diagonal(sum3, 0, 128, every), 64, 1)
    back4 = pltpu.roll(diagonal(sum4, 0, 128, every), 64, 1)
    groups = (
        diagonal(sum0, 0, 64, every) + jnp.where(lower, back2, back3),
        diagonal(sum1, 0, 64, every) + jnp.where(lower, back3, back4),
        jnp.where(lower, diagonal(sum2, 0, 64, (0, 1)) + back4, diagonal(sum2, 192, 128, (2, 3))),
        diagonal(sum3, 64, 128, every),
        diagonal(sum4, 64, 128, every),
    )
    for n, group in enumerate(groups):
        send2.reshape(512, 128)[pl.ds(n, 64, stride=8), :] = group

    def fourier_step(e, carry):
        lat = lax.rem(z + lax.div(e, 8), 8) * 8 + (rc ^ lax.rem(e, 8))
        row = jnp.where(lat < 32, lat, 95 - lat)
        src, dst = send2.at[row, pl.ds(0, 5), :], recv2.at[band, pl.ds(0, 5), :]

        @pl.when(lat != band)
        def _():
            pltpu.make_async_remote_copy(
                src_ref=src, dst_ref=dst, send_sem=ssem2, recv_sem=rsem2, device_id=(lat, lev), device_id_type=MESH
            ).start()

        @pl.when(lat == band)
        def _():
            pltpu.make_async_copy(src, dst, rsem2).start()

        return carry

    lax.fori_loop(0, 64, fourier_step, 0)
    arrived = recv2.at[:, pl.ds(0, 5), :]
    pltpu.make_async_copy(arrived, arrived, rsem2).wait()

    def received(n):
        return recv2.reshape(512, 128)[pl.ds(n, 64, stride=8), :].astype(BF16).astype(F32)

    first_two = jnp.concatenate([received(0), received(1)], axis=0).T
    second_two = jnp.concatenate([received(2), received(3)], axis=0).T
    last_one = received(4)
    last_one = jnp.concatenate([last_one, last_one], axis=0).T
    left = iota((16, 128), 1) < 64

    def coefficients(part):
        tiles = []
        for source in (first_two, second_two):
            for fine in range(4):
                at = fine * 32 + part * 16
                tiles.append(source[at : at + 16])
        for fine in (0, 2):
            at = fine * 32 + part * 16
            tiles.append(jnp.where(left, last_one[at : at + 16], last_one[at + 32 : at + 48]))
        return tiles

    reals, imags = coefficients(0), coefficients(1)

    def twist(start, count):
        for tile in range(10):
            cols = slice(tile * 128, tile * 128 + 128)
            imag_cols = slice(1280 + tile * 128, 1408 + tile * 128)
            cosines, sines = cos_t[pl.ds(start, 8), cols], sin_t[pl.ds(start, 8), cols]
            real, imag = reals[tile], imags[tile]
            for n in range(count):
                at = pl.ds(pl.multiple_of((start + n) * 16, 16), 16)
                cosine, sine = cosines[n : n + 1], sines[n : n + 1]
                tw[at, cols] = (real * cosine - imag * sine).astype(BF16)
                tw[at, imag_cols] = (real * sine + imag * cosine).astype(BF16)

    def twist_step(n, carry):
        twist(pl.multiple_of(n * 8, 8), 8)
        return carry

    lax.fori_loop(0, 5, twist_step, 0)
    twist(40, 1)

    result = dot_nn(tw[...], basis[...])
    for b in range(BLOCKS):
        inside = (iota((16, 128), 1) + 128 * b).astype(F32) < row_len
        width = min(128, LONMAX - 128 * b)
        for out, at in ((out_f, 0), (out_s, 128)):
            piece = jnp.where(inside, result[16 * b : 16 * b + 16, at : at + 128], 0.0)
            out[0, :, 128 * b : 128 * b + width] = piece[:, :width]

    @pl.when(own_line)
    def _():
        sent = send1.at[pl.ds(0, 63)]
        pltpu.make_async_copy(sent, sent, ssem1).wait()

    @pl.when(jnp.logical_not(own_line))
    def _():
        pltpu.make_async_copy(send1, send1, ssem1).wait()

    gone = send2.at[pl.ds(0, 63), pl.ds(0, 5), :]
    pltpu.make_async_copy(gone, gone, ssem2).wait()


def shards(control, vertical_root, legendre, wave_list, row_length):
    shape = jax.ShapeDtypeStruct((1, 16, LONMAX), F32)
    vmem, hbm = pl.BlockSpec(memory_space=pltpu.VMEM), pl.BlockSpec(memory_space=pl.ANY)
    return pl.pallas_call(
        kernel,
        out_shape=(shape, shape),
        in_specs=[hbm] * 5,
        out_specs=(vmem, vmem),
        scratch_shapes=[
            pltpu.VMEM((20, 320, 128), BF16),
            pltpu.VMEM((20, 128, 128), BF16),
            pltpu.SMEM((1280,), jnp.int32),
            pltpu.VMEM((640, 1280), BF16),
            pltpu.SMEM((32,), jnp.int32),
            pltpu.VMEM((32 * 320, 128), F32),
            pltpu.VMEM((64, 56, 128), BF16),
            pltpu.VMEM((64, 56, 128), BF16),
            pltpu.VMEM((512, 1024), BF16),
            pltpu.VMEM((896, 1024), BF16),
            pltpu.VMEM((1280, 1024), BF16),
            pltpu.VMEM((640, 1024), BF16),
            pltpu.VMEM((64, 8, 128), F32),
            pltpu.VMEM((64, 8, 128), F32),
            pltpu.VMEM((48, 1280), F32),
            pltpu.VMEM((48, 1280), F32),
            pltpu.VMEM((2560, 256), BF16),
            pltpu.VMEM((656, 2560), BF16),
            pltpu.SemaphoreType.DMA((5,)),
            pltpu.SemaphoreType.DMA,
            pltpu.SemaphoreType.DMA,
            pltpu.SemaphoreType.DMA,
            pltpu.SemaphoreType.DMA,
        ],
        compiler_params=pltpu.CompilerParams(
            collective_id=0, has_side_effects=True, vmem_limit_bytes=56 * 2**20
        ),
    )(
        control.reshape(20, 320, 128),
        vertical_root,
        legendre.reshape(640, 1280),
        wave_list,
        row_length,
    )


def solution(mesh):
    placed = (P("band", "lev", None, None), P("band", None, None), P("band", None, None), P(), P())
    return jax.shard_map(
        shards,
        mesh=mesh,
        in_specs=placed,
        out_specs=(P("band", "lev", None), P("band", "lev", None)),
        check_vma=False,
    )
```

```python
import functools

import jax
import jax.numpy as jnp
from jax import lax
from jax.experimental import pallas as pl
from jax.experimental.pallas import tpu as pltpu
from jax.sharding import PartitionSpec as P

M = 1280
LONMAX = 5136
BLOCKS = 41
F32 = jnp.float32
BF16 = jnp.bfloat16
MESH = pl.DeviceIdType.MESH

SIN_TERMS = (3.14159264, -5.16771008, 2.55007752, -0.598291286, 0.0776576603)
COS_TERMS = (0.999999953, -4.93479283, 4.05841135, -1.33187657, 0.219689611)


def iota(shape, dim):
    return lax.broadcasted_iota(jnp.int32, shape, dim)


def dot_nt(a, b):
    return lax.dot_general(a, b, (((1,), (1,)), ((), ())), preferred_element_type=F32)


def dot_nn(a, b):
    return lax.dot_general(a, b, (((1,), (0,)), ((), ())), preferred_element_type=F32)


def polynomial(terms, square):
    total = jnp.full_like(square, terms[-1])
    for term in terms[-2::-1]:
        total = total * square + term
    return total


def turn(product, row_len, inverse):
    doubled = product * 2.0
    halves = jnp.floor(doubled * inverse + 0.5)
    part = (doubled - halves * row_len) * inverse
    even = halves * 0.5
    sign = 1.0 - 4.0 * (even - jnp.floor(even))
    square = part * part
    return polynomial(COS_TERMS, square) * sign, polynomial(SIN_TERMS, square) * part * sign


def exchange(rows):
    group = lax.shift_right_logical(iota((8, 128), 1), 4)
    turned = [pltpu.roll(row, 16 * r, 1) if r else row for r, row in enumerate(rows)]
    for step in (1, 2, 4):
        odd = (group & step) != 0
        turned = [jnp.where(odd, turned[(n + step) % 8], turned[n]) for n in range(8)]
    found = [turned[(8 - y) % 8] for y in range(8)]
    return [pltpu.roll(row, 128 - 16 * y, 1) if y else row for y, row in enumerate(found)]


def kernel(
    ctrl_hbm, vert_hbm, leg_hbm, waves_hbm, rows_hbm,
    blocks,
    ctrl, vert, waves, leg, rows_len, prod, send1, recv1, w0, w1, w2, w3, send2, recv2, cos_t, sin_t, basis, tw,
    acc0, acc1, acc2, acc3,
    in_sem, ctrl_sem, vert_sem, ssem1, rsem1, ssem2, rsem2, told1, told2,
):
    band, lev = lax.axis_index("band"), lax.axis_index("lev")
    z, rc = lax.div(band, 8), lax.rem(band, 8)
    xpos, core = lax.div(rc, 2), lax.rem(rc, 2)
    own_line = z == lev

    def chunk_copies(q):
        rows = pl.ds(5 * q, 5)
        return (
            pltpu.make_async_copy(ctrl_hbm.at[rows], ctrl.at[rows], ctrl_sem.at[q]),
            pltpu.make_async_copy(vert_hbm.at[rows], vert.at[rows], vert_sem.at[q]),
        )

    copies = [
        pltpu.make_async_copy(src, dst, in_sem.at[n])
        for n, (src, dst) in enumerate(((waves_hbm, waves), (leg_hbm, leg), (rows_hbm, rows_len)))
    ]
    for q in range(4):
        for copy in chunk_copies(q):
            copy.start()
    for copy in copies:
        copy.start()

    barrier = pltpu.get_barrier_semaphore()

    def greet(e, carry):
        @pl.when(jnp.logical_not(jnp.logical_and(e == band, own_line)))
        def _():
            pl.semaphore_signal(barrier, inc=1, device_id=(e, z), device_id_type=MESH)

        return carry

    lax.fori_loop(0, 64, greet, 0)
    def products(q, carry):
        for copy in chunk_copies(q):
            copy.wait()
        for n in range(5):
            half = lax.div(q, 2)
            degree = 5 * q + n
            at = pl.multiple_of((degree + 6 * half) * 320, 8)
            prod[pl.ds(at, 320), :] = dot_nt(ctrl[degree], vert[degree])
        return carry

    lax.fori_loop(0, 4, products, 0)
    copies[0].wait()
    pl.semaphore_wait(barrier, jnp.where(own_line, 63, 64))

    def tell(sem, targets):
        for n, target in enumerate(targets):

            def signal(target=target):
                pl.semaphore_signal(sem, inc=1, device_id=target, device_id_type=MESH)

            if n:
                signal()
            else:
                pl.when(jnp.logical_not(own_line))(signal)

    tell(told1, [(lev * 8 + rc, lax.rem(lev + n, 8)) for n in range(8)])

    sub = iota((8, 128), 0)

    def owner_step(d, carry):
        owner = lax.rem(xpos + lax.div(d, 2), 4) * 2 + lax.rem(core + d, 2)
        base = waves[(lev * 8 + owner) * 20]
        first = owner * 40
        shift = 10 * band - base
        on_diagonal = shift == 0

        def load(half, k, row):
            return prod[pl.ds(first + ((16 * half + k) * 320 + row), 8, stride=320), :]

        def degrees(row, k):
            high = load(1, k, row)
            if row < 20:
                return high
            return jnp.where(sub + (k + shift) >= (row - 20) // 2, load(0, k, row - 20), high)

        def diagonal_row(row, place):
            if row < 20:
                return jnp.zeros((8, 128), F32)
            return jnp.where(on_diagonal, load(1, (row - 20) // 2 - place, row), 0.0)

        def extra_a(r):
            rows = jnp.where(sub < 6, diagonal_row(24 + r, 5), degrees(r, 2))
            rows = jnp.where(sub < 5, degrees(24 + r, 5), rows)
            rows = jnp.where(sub < 3, diagonal_row(32 + r, 2), rows)
            return jnp.where(sub < 2, degrees(32 + r, 8), rows)

        def extra_b(r):
            rows = jnp.where(sub < 5, degrees(8 + r, 5), 0.0)
            rows = jnp.where(sub < 3, diagonal_row(16 + r, 2), rows)
            return jnp.where(sub < 2, degrees(16 + r, 8), rows)

        def main(group):
            return exchange([degrees(8 * group + r, 0) for r in range(8)])

        for tile in range(3):
            top = main(2 * tile)
            low = main(2 * tile + 1) if tile < 2 else exchange([extra_a(r) for r in range(8)])
            for y in range(8):
                send1[8 * d + y, 16 * tile : 16 * tile + 16, :] = jnp.concatenate([top[y], low[y]], axis=0).astype(BF16)
        low = exchange([extra_b(r) for r in range(8)])
        for y in range(8):
            send1[8 * d + y, 48:56, :] = low[y].astype(BF16)

        for e in (4, 3, 5, 2, 6, 1, 7, 0):
            y = lax.rem(lev + e, 8)

            def send(y=y, e=e):
                pltpu.make_async_remote_copy(
                    src_ref=send1.at[8 * d + y], dst_ref=recv1.at[band], send_sem=ssem1, recv_sem=rsem1.at[z],
                    device_id=(lev * 8 + owner, y), device_id_type=MESH,
                ).start()

            if e > 0:
                send()
                continue
            mine = jnp.logical_and(own_line, d == 0)
            pl.when(jnp.logical_not(mine))(send)

            @pl.when(mine)
            def _(y=y):
                pltpu.make_async_copy(send1.at[8 * d + y], recv1.at[band], rsem1.at[z]).start()

        return carry

    lax.fori_loop(0, 8, owner_step, 0)

    copies[1].wait()
    copies[2].wait()
    own_base = waves[band * 20]
    lane = iota((32, 128), 1)
    slot = lane & 15
    alt = (1 - 2 * (lane & 1)).astype(F32)
    diag_lane = slot == 10
    zero = jnp.zeros((32, 128), F32)
    early8 = slot < 8

    def moved(part, by, low, high):
        return jnp.where(jnp.logical_and(slot >= low, slot <= high), pltpu.roll(part, by % 128, 1), zero)

    def weigh(bb, carry):
        start = pl.multiple_of(lax.div(bb * 5, 4) * 128, 128)
        cols = pl.ds(pl.multiple_of(bb * 128, 128), 128)
        pick_row, pick_lane = iota((256, 128), 0), iota((256, 128), 1)
        pick_slot = pick_lane & 15
        target = 32 * lax.rem(bb, 4) + 20 * lax.shift_right_logical(pick_lane, 4) + pick_slot
        valid = pick_slot < 10
        pick_low = jnp.where(jnp.logical_and(valid, pick_row == target), 1.0, 0.0).astype(BF16)
        pick_high = jnp.where(jnp.logical_and(valid, pick_row == target + 10), 1.0, 0.0).astype(BF16)
        high = dot_nn(leg[:, pl.ds(start, 256)], pick_high)
        low = dot_nn(leg[:320, pl.ds(start, 256)], pick_low)
        degree = 10 * (8 * bb + lax.shift_right_logical(lane, 4)) + slot

        def put(group, place, parts):
            for n, part in enumerate(parts):
                first8 = jnp.where(early8, part, zero)
                targets = (
                    ((w0, 0, first8), (w2, 1024, moved(part, 6, 14, 15))),
                    ((w0, 256, moved(part, 8, 8, 15)), (w3, 384, moved(part, -5, 3, 4))),
                    ((w1, 0, first8), (w3, 0, moved(part, -8, 0, 2))),
                    ((w1, 384, moved(part, 8, 8, 15)), (w2, 512, moved(part, 3, 11, 13))),
                    ((w2, 0, part),),
                )[group]
                for ref, start, value in targets:
                    ref[pl.ds(start + place + 32 * n, 32), cols] = value.astype(BF16)

        for i in range(10):
            sign = 1.0 - 2.0 * (i % 2)
            part = high[32 * i : 32 * i + 32]
            place = (i % 4) * 64
            put(i // 4, place, (part, part * (alt * -sign)))
        for i in range(10):
            sign = 1.0 - 2.0 * (i % 2)
            first = jnp.where(degree >= own_base + i, low[32 * i : 32 * i + 32], zero)
            part = high[320 + 32 * i : 352 + 32 * i]
            second = jnp.where(degree < own_base + i, part, zero)
            second = jnp.where(diag_lane, pltpu.roll(part, 10 - i, 1), second)
            signs = alt * sign
            place = 128 + i * 128 if i < 2 else ((i - 2) % 4) * 128
            put(
                (i + 2) // 4 + 2, place,
                (first, first * signs, second, second * jnp.where(diag_lane, 1.0, signs)),
            )
        return carry

    lax.fori_loop(0, 8, weigh, 0)
    pl.semaphore_wait(told1, jnp.where(own_line, 7, 8))
    tell(told2, [(lev * 8 + (rc ^ n), z) for n in range(8)])

    row_len = rows_len[jnp.where(band < 32, band, 63 - band)].astype(F32)
    inverse = 1.0 / jnp.full((1, 128), row_len, F32)
    one_lane = iota((1, 128), 1)

    def gather_base(o, found):
        return jnp.where((one_lane & 63) == o, waves[o * 20], found)

    bases = lax.fori_loop(0, 64, gather_base, jnp.zeros((1, 128), jnp.int32))
    half = lax.shift_right_logical(one_lane, 6)

    def tables(tile, carry):
        fine = lax.rem(tile, 4)
        pair = lax.div(tile, 4)
        slots = jnp.where(pair == 2, 16 + 2 * fine + half, 8 * pair + 4 * half + fine)
        wave = jnp.where(slots < 10, bases + slots, M - 1 - bases - (slots - 10)).astype(F32)
        cols = pl.ds(pl.multiple_of(tile * 128, 128), 128)
        starts = iota((48, 128), 0).astype(F32) * 128.0
        cosine, sine = turn(starts * wave, row_len, inverse)
        cos_t[:, cols] = cosine
        sin_t[:, cols] = sine
        columns = iota((128, 128), 0).astype(F32)
        cosine, sine = turn(columns * wave, row_len, inverse)
        weight = jnp.where(wave == 0.0, 1.0, 2.0)
        slope = weight * wave * (1.0 / M)
        real = pl.ds(pl.multiple_of(tile * 128, 128), 128)
        imag = pl.ds(pl.multiple_of(1280 + tile * 128, 128), 128)
        basis[real, :128] = (cosine * weight).T.astype(BF16)
        basis[imag, :128] = (sine * -weight).T.astype(BF16)
        basis[real, 128:] = (sine * -slope).T.astype(BF16)
        basis[imag, 128:] = (cosine * -slope).T.astype(BF16)
        return carry

    lax.fori_loop(0, 10, tables, 0)

    wide = iota((64, 128), 1)
    chunk = lax.shift_right_logical(wide, 5)

    def rows16(n, first, last):
        count = 16 * (last - first)
        if n < 3:
            return recv1[first:last, 16 * n : 16 * n + 16, :].reshape(count, 128)
        rest = recv1[first:last, 48:56, :]
        return jnp.concatenate([rest, jnp.zeros_like(rest)], axis=1).reshape(count, 128)

    def diagonal(value, start, step, where_chunks):
        total = None
        for n, at in enumerate(where_chunks):
            piece = value[start + step * n : start + step * n + 64]
            total = piece if total is None else jnp.where(chunk == at, piece, total)
        return total

    outs = None
    for first, last in ((0, 4), (4, 6), (6, 8)):
        for group in range(first, last):
            part = recv1.at[pl.ds(8 * group, 8)]
            pltpu.make_async_copy(part, part, rsem1.at[group]).wait()
        for n, acc in enumerate((acc0, acc1, acc2, acc3)):
            sums = dot_nn((w0, w1, w2, w3)[n][:, 128 * first : 128 * last], rows16(n, 8 * first, 8 * last))
            acc[...] = acc[...] + sums if first else sums
    out0, out1, out2, out3 = acc0[...], acc1[...], acc2[...], acc3[...]
    sum0 = out0[:256] + out2[1024:]
    sum1 = out0[256:] + out3[384:]
    sum2 = out1[:384] + out3[:384]
    sum3 = out1[384:] + out2[512:1024]
    sum4 = out2[:512]
    every = (0, 1, 2, 3)
    lower = wide < 64
    back2 = pltpu.roll(diagonal(sum2, 128, 128, (2, 3)), 64, 1)
    back3 = pltpu.roll(diagonal(sum3, 0, 128, every), 64, 1)
    back4 = pltpu.roll(diagonal(sum4, 0, 128, every), 64, 1)
    groups = (
        diagonal(sum0, 0, 64, every) + jnp.where(lower, back2, back3),
        diagonal(sum1, 0, 64, every) + jnp.where(lower, back3, back4),
        jnp.where(lower, diagonal(sum2, 0, 64, (0, 1)) + back4, diagonal(sum2, 192, 128, (2, 3))),
        diagonal(sum3, 64, 128, every),
        diagonal(sum4, 64, 128, every),
    )
    for n, group in enumerate(groups):
        send2.reshape(512, 128)[pl.ds(n, 64, stride=8), :] = group

    def fourier_row(lat):
        row = jnp.where(lat < 32, lat, 95 - lat)
        return send2.at[row, pl.ds(0, 5), :], recv2.at[band, pl.ds(0, 5), :]

    def fourier_step(e, carry):
        lat = lax.rem(z + 4 + 3 * lax.div(e, 8), 8) * 8 + (rc ^ lax.rem(e, 8))
        src, dst = fourier_row(lat)
        pltpu.make_async_remote_copy(
            src_ref=src, dst_ref=dst, send_sem=ssem2, recv_sem=rsem2, device_id=(lat, lev), device_id_type=MESH
        ).start()
        return carry

    pl.semaphore_wait(told2, jnp.where(own_line, 7, 8))
    src, dst = fourier_row(band)
    pltpu.make_async_copy(src, dst, rsem2).start()
    lax.fori_loop(0, 32, fourier_step, 0)
    lax.fori_loop(33, 64, fourier_step, 0)
    arrived = recv2.at[:, pl.ds(0, 5), :]
    pltpu.make_async_copy(arrived, arrived, rsem2).wait()

    def received(n):
        return recv2.reshape(512, 128)[pl.ds(n, 64, stride=8), :].astype(BF16).astype(F32)

    first_two = jnp.concatenate([received(0), received(1)], axis=0).T
    second_two = jnp.concatenate([received(2), received(3)], axis=0).T
    last_one = received(4)
    last_one = jnp.concatenate([last_one, last_one], axis=0).T
    left = iota((16, 128), 1) < 64

    def coefficients(part):
        tiles = []
        for source in (first_two, second_two):
            for fine in range(4):
                at = fine * 32 + part * 16
                tiles.append(source[at : at + 16])
        for fine in (0, 2):
            at = fine * 32 + part * 16
            tiles.append(jnp.where(left, last_one[at : at + 16], last_one[at + 32 : at + 48]))
        return tiles

    reals, imags = coefficients(0), coefficients(1)

    def twist(start, count):
        for tile in range(10):
            cols = slice(tile * 128, tile * 128 + 128)
            imag_cols = slice(1280 + tile * 128, 1408 + tile * 128)
            cosines, sines = cos_t[pl.ds(start, 8), cols], sin_t[pl.ds(start, 8), cols]
            real, imag = reals[tile], imags[tile]
            for n in range(count):
                at = pl.ds(pl.multiple_of((start + n) * 16, 16), 16)
                cosine, sine = cosines[n : n + 1], sines[n : n + 1]
                tw[at, cols] = (real * cosine - imag * sine).astype(BF16)
                tw[at, imag_cols] = (real * sine + imag * cosine).astype(BF16)

    def twist_step(n, carry):
        twist(pl.multiple_of(n * 8, 8), 8)
        return carry

    lax.fori_loop(0, 5, twist_step, 0)
    twist(40, 1)

    result = dot_nn(tw[...], basis[...])
    column = iota((16, 256), 1) & 127
    for b in range(BLOCKS):
        inside = (column + 128 * b).astype(F32) < row_len
        blocks[16 * b : 16 * b + 16, :] = jnp.where(inside, result[16 * b : 16 * b + 16], 0.0)

    @pl.when(own_line)
    def _():
        sent = send1.at[pl.ds(0, 63)]
        pltpu.make_async_copy(sent, sent, ssem1).wait()

    @pl.when(jnp.logical_not(own_line))
    def _():
        pltpu.make_async_copy(send1, send1, ssem1).wait()

    gone = send2.at[pl.ds(0, 63), pl.ds(0, 5), :]
    pltpu.make_async_copy(gone, gone, ssem2).wait()


def lay_out(blocks, out_f, out_s):
    for b in range(BLOCKS):
        width = min(128, LONMAX - 128 * b)
        for out, at in ((out_f, 0), (out_s, 128)):
            out[0, :, 128 * b : 128 * b + width] = blocks[16 * b : 16 * b + 16, at : at + width]


def shards(control, vertical_root, legendre, wave_list, row_length):
    shape = jax.ShapeDtypeStruct((1, 16, LONMAX), F32)
    vmem, hbm = pl.BlockSpec(memory_space=pltpu.VMEM), pl.BlockSpec(memory_space=pl.ANY)
    blocks = pl.pallas_call(
        kernel,
        out_shape=jax.ShapeDtypeStruct((16 * BLOCKS, 256), F32),
        in_specs=[hbm] * 5,
        out_specs=vmem,
        scratch_shapes=[
            pltpu.VMEM((20, 320, 128), BF16),
            pltpu.VMEM((20, 128, 128), BF16),
            pltpu.SMEM((1280,), jnp.int32),
            pltpu.VMEM((640, 1280), BF16),
            pltpu.SMEM((32,), jnp.int32),
            pltpu.VMEM((32 * 320, 128), F32),
            pltpu.VMEM((64, 56, 128), BF16),
            pltpu.VMEM((64, 56, 128), BF16),
            pltpu.VMEM((512, 1024), BF16),
            pltpu.VMEM((896, 1024), BF16),
            pltpu.VMEM((1280, 1024), BF16),
            pltpu.VMEM((640, 1024), BF16),
            pltpu.VMEM((64, 8, 128), F32),
            pltpu.VMEM((64, 8, 128), F32),
            pltpu.VMEM((48, 1280), F32),
            pltpu.VMEM((48, 1280), F32),
            pltpu.VMEM((2560, 256), BF16),
            pltpu.VMEM((656, 2560), BF16),
            pltpu.VMEM((512, 128), F32),
            pltpu.VMEM((896, 128), F32),
            pltpu.VMEM((1280, 128), F32),
            pltpu.VMEM((640, 128), F32),
            pltpu.SemaphoreType.DMA((3,)),
            pltpu.SemaphoreType.DMA((4,)),
            pltpu.SemaphoreType.DMA((4,)),
            pltpu.SemaphoreType.DMA,
            pltpu.SemaphoreType.DMA((8,)),
            pltpu.SemaphoreType.DMA,
            pltpu.SemaphoreType.DMA,
            pltpu.SemaphoreType.REGULAR,
            pltpu.SemaphoreType.REGULAR,
        ],
        compiler_params=pltpu.CompilerParams(
            collective_id=0, has_side_effects=True, vmem_limit_bytes=56 * 2**20
        ),
    )(
        control.reshape(20, 320, 128),
        vertical_root,
        legendre.reshape(640, 1280),
        wave_list,
        row_length,
    )
    return pl.pallas_call(
        lay_out, out_shape=(shape, shape), in_specs=[vmem], out_specs=(vmem, vmem)
    )(blocks)


def solution(mesh):
    placed = (P("band", "lev", None, None), P("band", None, None), P("band", None, None), P(), P())
    return jax.shard_map(
        shards,
        mesh=mesh,
        in_specs=placed,
        out_specs=(P("band", "lev", None), P("band", "lev", None)),
        check_vma=False,
    )
```

```python
import functools

import jax
import jax.numpy as jnp
from jax import lax
from jax.experimental import pallas as pl
from jax.experimental.pallas import tpu as pltpu
from jax.sharding import PartitionSpec as P

M = 1280
LONMAX = 5136
BLOCKS = 41
F32 = jnp.float32
BF16 = jnp.bfloat16
MESH = pl.DeviceIdType.MESH

SIN_TERMS = (3.14159264, -5.16771008, 2.55007752, -0.598291286, 0.0776576603)
COS_TERMS = (0.999999953, -4.93479283, 4.05841135, -1.33187657, 0.219689611)


def iota(shape, dim):
    return lax.broadcasted_iota(jnp.int32, shape, dim)


def dot_nt(a, b):
    return lax.dot_general(a, b, (((1,), (1,)), ((), ())), preferred_element_type=F32)


def dot_nn(a, b):
    return lax.dot_general(a, b, (((1,), (0,)), ((), ())), preferred_element_type=F32)


def polynomial(terms, square):
    total = jnp.full_like(square, terms[-1])
    for term in terms[-2::-1]:
        total = total * square + term
    return total


def turn(product, row_len, inverse):
    doubled = product * 2.0
    halves = jnp.floor(doubled * inverse + 0.5)
    part = (doubled - halves * row_len) * inverse
    even = halves * 0.5
    sign = 1.0 - 4.0 * (even - jnp.floor(even))
    square = part * part
    return polynomial(COS_TERMS, square) * sign, polynomial(SIN_TERMS, square) * part * sign


def exchange(rows):
    group = lax.shift_right_logical(iota((8, 128), 1), 4)
    turned = [pltpu.roll(row, 16 * r, 1) if r else row for r, row in enumerate(rows)]
    for step in (1, 2, 4):
        odd = (group & step) != 0
        turned = [jnp.where(odd, turned[(n + step) % 8], turned[n]) for n in range(8)]
    found = [turned[(8 - y) % 8] for y in range(8)]
    return [pltpu.roll(row, 128 - 16 * y, 1) if y else row for y, row in enumerate(found)]


def kernel(
    ctrl_hbm, vert_hbm, leg_hbm, waves_hbm, rows_hbm,
    blocks,
    ctrl, vert, waves, leg, rows_len, prod, send1, recv1, w0, w1, w2, w3, staged, send2, recv2, cos_t, sin_t, basis, tw,
    acc0, acc1, acc2, acc3, total_ref,
    in_sem, ctrl_sem, vert_sem, ssem1, rsem1, ssem2, rsem2, told1, told2,
):
    band, lev = lax.axis_index("band"), lax.axis_index("lev")
    z, rc = lax.div(band, 8), lax.rem(band, 8)
    xpos, core = lax.div(rc, 2), lax.rem(rc, 2)
    own_line = z == lev

    def chunk_copies(q):
        rows = pl.ds(5 * q, 5)
        return (
            pltpu.make_async_copy(ctrl_hbm.at[rows], ctrl.at[rows], ctrl_sem.at[q]),
            pltpu.make_async_copy(vert_hbm.at[rows], vert.at[rows], vert_sem.at[q]),
        )

    copies = [
        pltpu.make_async_copy(src, dst, in_sem.at[n])
        for n, (src, dst) in enumerate(((waves_hbm, waves), (leg_hbm, leg), (rows_hbm, rows_len)))
    ]
    for q in range(4):
        for copy in chunk_copies(q):
            copy.start()
    for copy in copies:
        copy.start()

    barrier = pltpu.get_barrier_semaphore()

    def greet(e, carry):
        @pl.when(jnp.logical_not(jnp.logical_and(e == band, own_line)))
        def _():
            pl.semaphore_signal(barrier, inc=1, device_id=(e, z), device_id_type=MESH)

        return carry

    lax.fori_loop(0, 64, greet, 0)
    def products(q, carry):
        for copy in chunk_copies(q):
            copy.wait()
        for n in range(5):
            half = lax.div(q, 2)
            degree = 5 * q + n
            at = pl.multiple_of((degree + 6 * half) * 320, 8)
            prod[pl.ds(at, 320), :] = dot_nt(ctrl[degree], vert[degree])
        return carry

    lax.fori_loop(0, 4, products, 0)
    copies[0].wait()
    pl.semaphore_wait(barrier, jnp.where(own_line, 63, 64))

    def tell(sem, targets):
        for n, target in enumerate(targets):

            def signal(target=target):
                pl.semaphore_signal(sem, inc=1, device_id=target, device_id_type=MESH)

            if n:
                signal()
            else:
                pl.when(jnp.logical_not(own_line))(signal)

    tell(told1, [(lev * 8 + rc, lax.rem(lev + n, 8)) for n in range(8)])

    sub = iota((8, 128), 0)

    def owner_step(d, carry):
        owner = lax.rem(xpos + lax.div(d, 2), 4) * 2 + lax.rem(core + d, 2)
        base = waves[(lev * 8 + owner) * 20]
        first = owner * 40
        shift = 10 * band - base
        on_diagonal = shift == 0

        def load(half, k, row):
            return prod[pl.ds(first + ((16 * half + k) * 320 + row), 8, stride=320), :]

        def degrees(row, k):
            high = load(1, k, row)
            if row < 20:
                return high
            return jnp.where(sub + (k + shift) >= (row - 20) // 2, load(0, k, row - 20), high)

        def diagonal_row(row, place):
            if row < 20:
                return jnp.zeros((8, 128), F32)
            return jnp.where(on_diagonal, load(1, (row - 20) // 2 - place, row), 0.0)

        def extra_a(r):
            rows = jnp.where(sub < 6, diagonal_row(24 + r, 5), degrees(r, 2))
            rows = jnp.where(sub < 5, degrees(24 + r, 5), rows)
            rows = jnp.where(sub < 3, diagonal_row(32 + r, 2), rows)
            return jnp.where(sub < 2, degrees(32 + r, 8), rows)

        def extra_b(r):
            rows = jnp.where(sub < 5, degrees(8 + r, 5), 0.0)
            rows = jnp.where(sub < 3, diagonal_row(16 + r, 2), rows)
            return jnp.where(sub < 2, degrees(16 + r, 8), rows)

        def main(group):
            return exchange([degrees(8 * group + r, 0) for r in range(8)])

        for tile in range(3):
            top = main(2 * tile)
            low = main(2 * tile + 1) if tile < 2 else exchange([extra_a(r) for r in range(8)])
            for y in range(8):
                send1[8 * d + y, 16 * tile : 16 * tile + 16, :] = jnp.concatenate([top[y], low[y]], axis=0).astype(BF16)
        low = exchange([extra_b(r) for r in range(8)])
        for y in range(8):
            send1[8 * d + y, 48:56, :] = low[y].astype(BF16)

        for e in (4, 3, 5, 2, 6, 1, 7, 0):
            y = lax.rem(lev + e, 8)

            def send(y=y, e=e):
                pltpu.make_async_remote_copy(
                    src_ref=send1.at[8 * d + y], dst_ref=recv1.at[band], send_sem=ssem1, recv_sem=rsem1.at[z],
                    device_id=(lev * 8 + owner, y), device_id_type=MESH,
                ).start()

            if e > 0:
                send()
                continue
            mine = jnp.logical_and(own_line, d == 0)
            pl.when(jnp.logical_not(mine))(send)

            @pl.when(mine)
            def _(y=y):
                pltpu.make_async_copy(send1.at[8 * d + y], recv1.at[band], rsem1.at[z]).start()

        return carry

    lax.fori_loop(0, 8, owner_step, 0)

    copies[1].wait()
    copies[2].wait()
    own_base = waves[band * 20]
    lane = iota((32, 128), 1)
    slot = lane & 15
    alt = (1 - 2 * (lane & 1)).astype(F32)
    diag_lane = slot == 10
    zero = jnp.zeros((32, 128), F32)
    early8 = slot < 8

    def moved(part, by, low, high):
        return jnp.where(jnp.logical_and(slot >= low, slot <= high), pltpu.roll(part, by % 128, 1), zero)

    def weigh(bb, carry):
        start = pl.multiple_of(lax.div(bb * 5, 4) * 128, 128)
        cols = pl.ds(pl.multiple_of(bb * 128, 128), 128)
        pick_row, pick_lane = iota((256, 128), 0), iota((256, 128), 1)
        pick_slot = pick_lane & 15
        target = 32 * lax.rem(bb, 4) + 20 * lax.shift_right_logical(pick_lane, 4) + pick_slot
        valid = pick_slot < 10
        pick_low = jnp.where(jnp.logical_and(valid, pick_row == target), 1.0, 0.0).astype(BF16)
        pick_high = jnp.where(jnp.logical_and(valid, pick_row == target + 10), 1.0, 0.0).astype(BF16)
        high = dot_nn(leg[:, pl.ds(start, 256)], pick_high)
        low = dot_nn(leg[:320, pl.ds(start, 256)], pick_low)
        degree = 10 * (8 * bb + lax.shift_right_logical(lane, 4)) + slot

        def put(group, place, parts):
            for n, part in enumerate(parts):
                first8 = jnp.where(early8, part, zero)
                targets = (
                    ((w0, 0, first8), (w2, 1024, moved(part, 6, 14, 15))),
                    ((w0, 256, moved(part, 8, 8, 15)), (w3, 384, moved(part, -5, 3, 4))),
                    ((w1, 0, first8), (w3, 0, moved(part, -8, 0, 2))),
                    ((w1, 384, moved(part, 8, 8, 15)), (w2, 512, moved(part, 3, 11, 13))),
                    ((w2, 0, part),),
                )[group]
                for ref, start, value in targets:
                    ref[pl.ds(start + place + 32 * n, 32), cols] = value.astype(BF16)

        for i in range(10):
            sign = 1.0 - 2.0 * (i % 2)
            part = high[32 * i : 32 * i + 32]
            place = (i % 4) * 64
            put(i // 4, place, (part, part * (alt * -sign)))
        for i in range(10):
            sign = 1.0 - 2.0 * (i % 2)
            first = jnp.where(degree >= own_base + i, low[32 * i : 32 * i + 32], zero)
            part = high[320 + 32 * i : 352 + 32 * i]
            second = jnp.where(degree < own_base + i, part, zero)
            second = jnp.where(diag_lane, pltpu.roll(part, 10 - i, 1), second)
            signs = alt * sign
            place = 128 + i * 128 if i < 2 else ((i - 2) % 4) * 128
            put(
                (i + 2) // 4 + 2, place,
                (first, first * signs, second, second * jnp.where(diag_lane, 1.0, signs)),
            )
        return carry

    lax.fori_loop(0, 8, weigh, 0)
    pl.semaphore_wait(told1, jnp.where(own_line, 7, 8))
    tell(told2, [(lev * 8 + (rc ^ n), z) for n in range(8)])

    row_len = rows_len[jnp.where(band < 32, band, 63 - band)].astype(F32)
    inverse = 1.0 / jnp.full((1, 128), row_len, F32)
    one_lane = iota((1, 128), 1)

    def gather_base(o, found):
        mine = (one_lane & 31) == o
        return tuple(jnp.where(mine, waves[(32 * h + o) * 20], found[h]) for h in range(2))

    no_base = jnp.zeros((1, 128), jnp.int32)
    bases = lax.fori_loop(0, 32, gather_base, (no_base, no_base))
    quarter = lax.shift_right_logical(one_lane, 5)

    def tables(tile, carry):
        part = lax.div(tile, 5)
        fine = lax.rem(tile, 5)
        base = jnp.where(part == 0, bases[0], bases[1])
        slots = jnp.where(fine == 4, 16 + quarter, 4 * quarter + fine)
        wave = jnp.where(slots < 10, base + slots, M - 1 - base - (slots - 10)).astype(F32)
        cols = pl.ds(pl.multiple_of(tile * 128, 128), 128)
        starts = iota((48, 128), 0).astype(F32) * 128.0
        cosine, sine = turn(starts * wave, row_len, inverse)
        cos_t[:, cols] = cosine
        sin_t[:, cols] = sine
        columns = iota((128, 128), 0).astype(F32)
        cosine, sine = turn(columns * wave, row_len, inverse)
        weight = jnp.where(wave == 0.0, 1.0, 2.0)
        slope = weight * wave * (1.0 / M)
        real = pl.ds(pl.multiple_of((tile + 5 * part) * 128, 128), 128)
        imag = pl.ds(pl.multiple_of((tile + 5 * part + 5) * 128, 128), 128)
        basis[real, :128] = (cosine * weight).T.astype(BF16)
        basis[imag, :128] = (sine * -weight).T.astype(BF16)
        basis[real, 128:] = (sine * -slope).T.astype(BF16)
        basis[imag, 128:] = (cosine * -slope).T.astype(BF16)
        return carry

    lax.fori_loop(0, 10, tables, 0)

    wide = iota((64, 128), 1)
    chunk = lax.shift_right_logical(wide, 5)

    def rows16(n, first, last):
        count = 16 * (last - first)
        if n < 3:
            return recv1[first:last, 16 * n : 16 * n + 16, :].reshape(count, 128)
        rest = recv1[first:last, 48:56, :]
        return jnp.concatenate([rest, jnp.zeros_like(rest)], axis=1).reshape(count, 128)

    def diagonal(value, start, step, where_chunks):
        total = None
        for n, at in enumerate(where_chunks):
            piece = value[start + step * n : start + step * n + 64]
            total = piece if total is None else jnp.where(chunk == at, piece, total)
        return total

    outs = None
    for first, last in ((0, 4), (4, 6), (6, 8)):
        for group in range(first, last):
            part = recv1.at[pl.ds(8 * group, 8)]
            pltpu.make_async_copy(part, part, rsem1.at[group]).wait()
        for n, acc in enumerate((acc0, acc1, acc2, acc3)):
            sums = dot_nn((w0, w1, w2, w3)[n][:, 128 * first : 128 * last], rows16(n, 8 * first, 8 * last))
            acc[...] = acc[...] + sums if first else sums
    out0, out1, out2, out3 = acc0[...], acc1[...], acc2[...], acc3[...]
    sum0 = out0[:256] + out2[1024:]
    sum1 = out0[256:] + out3[384:]
    sum2 = out1[:384] + out3[:384]
    sum3 = out1[384:] + out2[512:1024]
    sum4 = out2[:512]
    every = (0, 1, 2, 3)
    lower = wide < 64
    back2 = pltpu.roll(diagonal(sum2, 128, 128, (2, 3)), 64, 1)
    back3 = pltpu.roll(diagonal(sum3, 0, 128, every), 64, 1)
    back4 = pltpu.roll(diagonal(sum4, 0, 128, every), 64, 1)
    groups = (
        diagonal(sum0, 0, 64, every) + jnp.where(lower, back2, back3),
        diagonal(sum1, 0, 64, every) + jnp.where(lower, back3, back4),
        jnp.where(lower, diagonal(sum2, 0, 64, (0, 1)) + back4, diagonal(sum2, 192, 128, (2, 3))),
        diagonal(sum3, 64, 128, every),
        diagonal(sum4, 64, 128, every),
    )
    for n, group in enumerate(groups):
        staged.reshape(512, 128)[pl.ds(n, 64, stride=8), :] = group
    staged.reshape(512, 128)[pl.ds(5, 64, stride=8), :] = jnp.zeros((64, 128), F32)
    send2[...] = staged[:, :6, :].astype(BF16)

    def fourier_row(lat):
        row = jnp.where(lat < 32, lat, 95 - lat)
        return send2.at[row], recv2.at[band]

    def fourier_step(n, carry):
        plane = lax.rem(z + 4 + 3 * n, 8)
        for e in range(8):
            lat = plane * 8 + (rc ^ e)
            src, dst = fourier_row(lat)
            copy = pltpu.make_async_remote_copy(
                src_ref=src, dst_ref=dst, send_sem=ssem2, recv_sem=rsem2.at[half],
                device_id=(lat, lev), device_id_type=MESH,
            )
            if e:
                copy.start()
            else:
                pl.when(n != 4)(copy.start)
        return carry

    half = lax.div(band, 32)
    pl.semaphore_wait(told2, jnp.where(own_line, 7, 8))
    src, dst = fourier_row(band)
    pltpu.make_async_copy(src, dst, rsem2.at[half]).start()
    lax.fori_loop(0, 8, fourier_step, 0)
    chunk16 = lax.shift_right_logical(iota((16, 128), 1), 5)
    for part in range(2):
        arrived = recv2.at[pl.ds(32 * part, 32)]
        pltpu.make_async_copy(arrived, arrived, rsem2.at[part]).wait()
        staged[32 * part : 32 * part + 32, :6, :] = recv2[32 * part : 32 * part + 32].astype(F32)

        def received(n):
            rows = pl.ds(256 * part + n, 32, stride=8)
            return staged.reshape(512, 128)[rows, :]

        four = jnp.concatenate([received(n) for n in range(4)], axis=0).T
        last = jnp.concatenate([received(4)] * 4, axis=0).T

        def coefficients(c):
            tiles = [four[32 * n + 16 * c : 32 * n + 16 * c + 16] for n in range(4)]
            mixed = last[16 * c : 16 * c + 16]
            for n in range(1, 4):
                mixed = jnp.where(chunk16 == n, last[32 * n + 16 * c : 32 * n + 16 * c + 16], mixed)
            return tiles + [mixed]

        reals, imags = coefficients(0), coefficients(1)

        def twist(start, count):
            for tile in range(5):
                cols = slice((5 * part + tile) * 128, (5 * part + tile) * 128 + 128)
                real_cols = slice((10 * part + tile) * 128, (10 * part + tile) * 128 + 128)
                imag_cols = slice((10 * part + tile + 5) * 128, (10 * part + tile + 5) * 128 + 128)
                cosines, sines = cos_t[pl.ds(start, 8), cols], sin_t[pl.ds(start, 8), cols]
                real, imag = reals[tile], imags[tile]
                for n in range(count):
                    at = pl.ds(pl.multiple_of((start + n) * 16, 16), 16)
                    cosine, sine = cosines[n : n + 1], sines[n : n + 1]
                    tw[at, real_cols] = (real * cosine - imag * sine).astype(BF16)
                    tw[at, imag_cols] = (real * sine + imag * cosine).astype(BF16)

        def twist_step(n, carry):
            twist(pl.multiple_of(n * 8, 8), 8)
            return carry

        lax.fori_loop(0, 5, twist_step, 0)
        twist(40, 1)
        sums = dot_nn(tw[:, 1280 * part : 1280 * part + 1280], basis[1280 * part : 1280 * part + 1280, :])
        if part == 0:
            total_ref[...] = sums
        else:
            total = sums

    column = iota((16, 256), 1) & 127
    for b in range(BLOCKS):
        inside = (column + 128 * b).astype(F32) < row_len
        blocks[16 * b : 16 * b + 16, :] = jnp.where(inside, total[16 * b : 16 * b + 16] + total_ref[16 * b : 16 * b + 16, :], 0.0)

    @pl.when(own_line)
    def _():
        sent = send1.at[pl.ds(0, 63)]
        pltpu.make_async_copy(sent, sent, ssem1).wait()

    @pl.when(jnp.logical_not(own_line))
    def _():
        pltpu.make_async_copy(send1, send1, ssem1).wait()

    gone = send2.at[pl.ds(0, 63)]
    pltpu.make_async_copy(gone, gone, ssem2).wait()


def lay_out(blocks, out_f, out_s):
    for b in range(BLOCKS):
        width = min(128, LONMAX - 128 * b)
        for out, at in ((out_f, 0), (out_s, 128)):
            out[0, :, 128 * b : 128 * b + width] = blocks[16 * b : 16 * b + 16, at : at + width]


def shards(control, vertical_root, legendre, wave_list, row_length):
    shape = jax.ShapeDtypeStruct((1, 16, LONMAX), F32)
    vmem, hbm = pl.BlockSpec(memory_space=pltpu.VMEM), pl.BlockSpec(memory_space=pl.ANY)
    blocks = pl.pallas_call(
        kernel,
        out_shape=jax.ShapeDtypeStruct((16 * BLOCKS, 256), F32),
        in_specs=[hbm] * 5,
        out_specs=vmem,
        scratch_shapes=[
            pltpu.VMEM((20, 320, 128), BF16),
            pltpu.VMEM((20, 128, 128), BF16),
            pltpu.SMEM((1280,), jnp.int32),
            pltpu.VMEM((640, 1280), BF16),
            pltpu.SMEM((32,), jnp.int32),
            pltpu.VMEM((32 * 320, 128), F32),
            pltpu.VMEM((64, 56, 128), BF16),
            pltpu.VMEM((64, 56, 128), BF16),
            pltpu.VMEM((512, 1024), BF16),
            pltpu.VMEM((896, 1024), BF16),
            pltpu.VMEM((1280, 1024), BF16),
            pltpu.VMEM((640, 1024), BF16),
            pltpu.VMEM((64, 8, 128), F32),
            pltpu.VMEM((64, 6, 128), BF16),
            pltpu.VMEM((64, 6, 128), BF16),
            pltpu.VMEM((48, 1280), F32),
            pltpu.VMEM((48, 1280), F32),
            pltpu.VMEM((2560, 256), BF16),
            pltpu.VMEM((656, 2560), BF16),
            pltpu.VMEM((512, 128), F32),
            pltpu.VMEM((896, 128), F32),
            pltpu.VMEM((1280, 128), F32),
            pltpu.VMEM((640, 128), F32),
            pltpu.VMEM((656, 256), F32),
            pltpu.SemaphoreType.DMA((3,)),
            pltpu.SemaphoreType.DMA((4,)),
            pltpu.SemaphoreType.DMA((4,)),
            pltpu.SemaphoreType.DMA,
            pltpu.SemaphoreType.DMA((8,)),
            pltpu.SemaphoreType.DMA,
            pltpu.SemaphoreType.DMA((2,)),
            pltpu.SemaphoreType.REGULAR,
            pltpu.SemaphoreType.REGULAR,
        ],
        compiler_params=pltpu.CompilerParams(
            collective_id=0, has_side_effects=True, vmem_limit_bytes=56 * 2**20
        ),
    )(
        control.reshape(20, 320, 128),
        vertical_root,
        legendre.reshape(640, 1280),
        wave_list,
        row_length,
    )
    return pl.pallas_call(
        lay_out, out_shape=(shape, shape), in_specs=[vmem], out_specs=(vmem, vmem)
    )(blocks)


def solution(mesh):
    placed = (P("band", "lev", None, None), P("band", None, None), P("band", None, None), P(), P())
    return jax.shard_map(
        shards,
        mesh=mesh,
        in_specs=placed,
        out_specs=(P("band", "lev", None), P("band", "lev", None)),
        check_vma=False,
    )
```

```python
import functools

import jax
import jax.numpy as jnp
from jax import lax
from jax.experimental import pallas as pl
from jax.experimental.pallas import tpu as pltpu
from jax.sharding import PartitionSpec as P

M = 1280
LONMAX = 5136
BLOCKS = 41
F32 = jnp.float32
BF16 = jnp.bfloat16
MESH = pl.DeviceIdType.MESH

SIN_TERMS = (3.14159264, -5.16771008, 2.55007752, -0.598291286, 0.0776576603)
COS_TERMS = (0.999999953, -4.93479283, 4.05841135, -1.33187657, 0.219689611)


def iota(shape, dim):
    return lax.broadcasted_iota(jnp.int32, shape, dim)


def dot_nt(a, b):
    return lax.dot_general(a, b, (((1,), (1,)), ((), ())), preferred_element_type=F32)


def dot_nn(a, b):
    return lax.dot_general(a, b, (((1,), (0,)), ((), ())), preferred_element_type=F32)


def polynomial(terms, square):
    total = jnp.full_like(square, terms[-1])
    for term in terms[-2::-1]:
        total = total * square + term
    return total


def turn(product, row_len, inverse):
    doubled = product * 2.0
    halves = jnp.floor(doubled * inverse + 0.5)
    part = (doubled - halves * row_len) * inverse
    even = halves * 0.5
    sign = 1.0 - 4.0 * (even - jnp.floor(even))
    square = part * part
    return polynomial(COS_TERMS, square) * sign, polynomial(SIN_TERMS, square) * part * sign


def exchange(rows):
    group = lax.shift_right_logical(iota((8, 128), 1), 4)
    turned = [pltpu.roll(row, 16 * r, 1) if r else row for r, row in enumerate(rows)]
    for step in (1, 2, 4):
        odd = (group & step) != 0
        turned = [jnp.where(odd, turned[(n + step) % 8], turned[n]) for n in range(8)]
    found = [turned[(8 - y) % 8] for y in range(8)]
    return [pltpu.roll(row, 128 - 16 * y, 1) if y else row for y, row in enumerate(found)]


def kernel(
    ctrl_hbm, vert_hbm, leg_hbm, waves_hbm, rows_hbm,
    blocks,
    ctrl, vert, waves, leg, rows_len, prod, send1, recv1, w0, w1, w2, w3, staged, send2, recv2, cos_t, sin_t, basis, tw,
    acc0, acc1, acc2, acc3, total_ref,
    in_sem, ctrl_sem, vert_sem, ssem1, rsem1, ssem2, rsem2, told1, told2,
):
    band, lev = lax.axis_index("band"), lax.axis_index("lev")
    z, rc = lax.div(band, 8), lax.rem(band, 8)
    xpos, core = lax.div(rc, 2), lax.rem(rc, 2)
    own_line = z == lev

    def chunk_copies(q):
        rows = pl.ds(5 * q, 5)
        return (
            pltpu.make_async_copy(ctrl_hbm.at[rows], ctrl.at[rows], ctrl_sem.at[q]),
            pltpu.make_async_copy(vert_hbm.at[rows], vert.at[rows], vert_sem.at[q]),
        )

    copies = [
        pltpu.make_async_copy(src, dst, in_sem.at[n])
        for n, (src, dst) in enumerate(((waves_hbm, waves), (leg_hbm, leg), (rows_hbm, rows_len)))
    ]
    barrier = pltpu.get_barrier_semaphore()

    def greet(e, carry):
        @pl.when(jnp.logical_not(jnp.logical_and(e == band, own_line)))
        def _():
            pl.semaphore_signal(barrier, inc=1, device_id=(e, z), device_id_type=MESH)

        return carry

    lax.fori_loop(0, 64, greet, 0)
    for q in range(4):
        for copy in chunk_copies(q):
            copy.start()
    for copy in copies:
        copy.start()

    def products(q, carry):
        for copy in chunk_copies(q):
            copy.wait()
        for n in range(5):
            half = lax.div(q, 2)
            degree = 5 * q + n
            at = pl.multiple_of((degree + 6 * half) * 320, 8)
            prod[pl.ds(at, 320), :] = dot_nt(ctrl[degree], vert[degree])
        return carry

    lax.fori_loop(0, 4, products, 0)
    copies[0].wait()
    pl.semaphore_wait(barrier, jnp.where(own_line, 63, 64))

    def tell(sem, targets):
        for n, target in enumerate(targets):

            def signal(target=target):
                pl.semaphore_signal(sem, inc=1, device_id=target, device_id_type=MESH)

            if n:
                signal()
            else:
                pl.when(jnp.logical_not(own_line))(signal)

    tell(told1, [(lev * 8 + rc, lax.rem(lev + n, 8)) for n in range(8)])

    sub = iota((8, 128), 0)

    def owner_step(d, carry):
        owner = lax.rem(xpos + lax.div(d, 2), 4) * 2 + lax.rem(core + d, 2)
        base = waves[(lev * 8 + owner) * 20]
        first = owner * 40
        shift = 10 * band - base
        on_diagonal = shift == 0

        def load(half, k, row):
            return prod[pl.ds(first + ((16 * half + k) * 320 + row), 8, stride=320), :]

        def degrees(row, k):
            high = load(1, k, row)
            if row < 20:
                return high
            return jnp.where(sub + (k + shift) >= (row - 20) // 2, load(0, k, row - 20), high)

        def diagonal_row(row, place):
            if row < 20:
                return jnp.zeros((8, 128), F32)
            return jnp.where(on_diagonal, load(1, (row - 20) // 2 - place, row), 0.0)

        def extra_a(r):
            rows = jnp.where(sub < 6, diagonal_row(24 + r, 5), degrees(r, 2))
            rows = jnp.where(sub < 5, degrees(24 + r, 5), rows)
            rows = jnp.where(sub < 3, diagonal_row(32 + r, 2), rows)
            return jnp.where(sub < 2, degrees(32 + r, 8), rows)

        def extra_b(r):
            rows = jnp.where(sub < 5, degrees(8 + r, 5), 0.0)
            rows = jnp.where(sub < 3, diagonal_row(16 + r, 2), rows)
            return jnp.where(sub < 2, degrees(16 + r, 8), rows)

        def main(group):
            return exchange([degrees(8 * group + r, 0) for r in range(8)])

        for tile in range(3):
            top = main(2 * tile)
            low = main(2 * tile + 1) if tile < 2 else exchange([extra_a(r) for r in range(8)])
            for y in range(8):
                send1[8 * d + y, 16 * tile : 16 * tile + 16, :] = jnp.concatenate([top[y], low[y]], axis=0).astype(BF16)
        low = exchange([extra_b(r) for r in range(8)])
        for y in range(8):
            send1[8 * d + y, 48:54, :] = low[y][:6].astype(BF16)

        for e in (4, 3, 5, 2, 6, 1, 7, 0):
            y = lax.rem(lev + e, 8)

            def send(y=y, e=e):
                pltpu.make_async_remote_copy(
                    src_ref=send1.at[8 * d + y], dst_ref=recv1.at[band], send_sem=ssem1, recv_sem=rsem1.at[z],
                    device_id=(lev * 8 + owner, y), device_id_type=MESH,
                ).start()

            if e > 0:
                send()
                continue
            mine = jnp.logical_and(own_line, d == 0)
            pl.when(jnp.logical_not(mine))(send)

            @pl.when(mine)
            def _(y=y):
                pltpu.make_async_copy(send1.at[8 * d + y], recv1.at[band], rsem1.at[z]).start()

        return carry

    lax.fori_loop(0, 8, owner_step, 0)

    copies[1].wait()
    copies[2].wait()
    own_base = waves[band * 20]
    lane = iota((32, 128), 1)
    slot = lane & 15
    alt = (1 - 2 * (lane & 1)).astype(F32)
    diag_lane = slot == 10
    zero = jnp.zeros((32, 128), F32)
    early8 = slot < 8

    def moved(part, by, low, high):
        return jnp.where(jnp.logical_and(slot >= low, slot <= high), pltpu.roll(part, by % 128, 1), zero)

    def weigh(bb, carry):
        start = pl.multiple_of(lax.div(bb * 5, 4) * 128, 128)
        cols = pl.ds(pl.multiple_of(bb * 128, 128), 128)
        pick_row, pick_lane = iota((256, 128), 0), iota((256, 128), 1)
        pick_slot = pick_lane & 15
        target = 32 * lax.rem(bb, 4) + 20 * lax.shift_right_logical(pick_lane, 4) + pick_slot
        valid = pick_slot < 10
        pick_low = jnp.where(jnp.logical_and(valid, pick_row == target), 1.0, 0.0).astype(BF16)
        pick_high = jnp.where(jnp.logical_and(valid, pick_row == target + 10), 1.0, 0.0).astype(BF16)
        high = dot_nn(leg[:, pl.ds(start, 256)], pick_high)
        low = dot_nn(leg[:320, pl.ds(start, 256)], pick_low)
        degree = 10 * (8 * bb + lax.shift_right_logical(lane, 4)) + slot

        def put(group, place, parts):
            for n, part in enumerate(parts):
                first8 = jnp.where(early8, part, zero)
                targets = (
                    ((w0, 0, first8), (w2, 1024, moved(part, 6, 14, 15))),
                    ((w0, 256, moved(part, 8, 8, 15)), (w3, 384, moved(part, -5, 3, 4))),
                    ((w1, 0, first8), (w3, 0, moved(part, -8, 0, 2))),
                    ((w1, 384, moved(part, 8, 8, 15)), (w2, 512, moved(part, 3, 11, 13))),
                    ((w2, 0, part),),
                )[group]
                for ref, start, value in targets:
                    ref[pl.ds(start + place + 32 * n, 32), cols] = value.astype(BF16)

        for i in range(10):
            sign = 1.0 - 2.0 * (i % 2)
            part = high[32 * i : 32 * i + 32]
            place = (i % 4) * 64
            put(i // 4, place, (part, part * (alt * -sign)))
        for i in range(10):
            sign = 1.0 - 2.0 * (i % 2)
            first = jnp.where(degree >= own_base + i, low[32 * i : 32 * i + 32], zero)
            part = high[320 + 32 * i : 352 + 32 * i]
            second = jnp.where(degree < own_base + i, part, zero)
            second = jnp.where(diag_lane, pltpu.roll(part, 10 - i, 1), second)
            signs = alt * sign
            place = 128 + i * 128 if i < 2 else ((i - 2) % 4) * 128
            put(
                (i + 2) // 4 + 2, place,
                (first, first * signs, second, second * jnp.where(diag_lane, 1.0, signs)),
            )
        return carry

    lax.fori_loop(0, 8, weigh, 0)
    pl.semaphore_wait(told1, jnp.where(own_line, 7, 8))
    tell(told2, [(lev * 8 + (rc ^ n), z) for n in range(8)])

    row_len = rows_len[jnp.where(band < 32, band, 63 - band)].astype(F32)
    inverse = 1.0 / jnp.full((1, 128), row_len, F32)
    one_lane = iota((1, 128), 1)

    def gather_base(o, found):
        mine = (one_lane & 31) == o
        return tuple(jnp.where(mine, waves[(32 * h + o) * 20], found[h]) for h in range(2))

    no_base = jnp.zeros((1, 128), jnp.int32)
    bases = lax.fori_loop(0, 32, gather_base, (no_base, no_base))
    quarter = lax.shift_right_logical(one_lane, 5)

    def tables(tile, carry):
        part = lax.div(tile, 5)
        fine = lax.rem(tile, 5)
        base = jnp.where(part == 0, bases[0], bases[1])
        slots = jnp.where(fine == 4, 16 + quarter, 4 * quarter + fine)
        wave = jnp.where(slots < 10, base + slots, M - 1 - base - (slots - 10)).astype(F32)
        cols = pl.ds(pl.multiple_of(tile * 128, 128), 128)
        starts = iota((48, 128), 0).astype(F32) * 128.0
        cosine, sine = turn(starts * wave, row_len, inverse)
        cos_t[:, cols] = cosine
        sin_t[:, cols] = sine
        columns = iota((128, 128), 0).astype(F32)
        cosine, sine = turn(columns * wave, row_len, inverse)
        weight = jnp.where(wave == 0.0, 1.0, 2.0)
        slope = weight * wave * (1.0 / M)
        real = pl.ds(pl.multiple_of((tile + 5 * part) * 128, 128), 128)
        imag = pl.ds(pl.multiple_of((tile + 5 * part + 5) * 128, 128), 128)
        basis[real, :128] = (cosine * weight).T.astype(BF16)
        basis[imag, :128] = (sine * -weight).T.astype(BF16)
        basis[real, 128:] = (sine * -slope).T.astype(BF16)
        basis[imag, 128:] = (cosine * -slope).T.astype(BF16)
        return carry

    lax.fori_loop(0, 10, tables, 0)

    wide = iota((64, 128), 1)
    chunk = lax.shift_right_logical(wide, 5)

    def rows16(n, first, last):
        count = 16 * (last - first)
        if n < 3:
            return recv1[first:last, 16 * n : 16 * n + 16, :].reshape(count, 128)
        rest = recv1[first:last, 48:54, :]
        return jnp.concatenate([rest, jnp.zeros((last - first, 10, 128), BF16)], axis=1).reshape(count, 128)

    def diagonal(value, start, step, where_chunks):
        total = None
        for n, at in enumerate(where_chunks):
            piece = value[start + step * n : start + step * n + 64]
            total = piece if total is None else jnp.where(chunk == at, piece, total)
        return total

    outs = None
    for first, last in ((0, 4), (4, 6), (6, 8)):
        for group in range(first, last):
            part = recv1.at[pl.ds(8 * group, 8)]
            pltpu.make_async_copy(part, part, rsem1.at[group]).wait()
        for n, acc in enumerate((acc0, acc1, acc2, acc3)):
            sums = dot_nn((w0, w1, w2, w3)[n][:, 128 * first : 128 * last], rows16(n, 8 * first, 8 * last))
            acc[...] = acc[...] + sums if first else sums
    out0, out1, out2, out3 = acc0[...], acc1[...], acc2[...], acc3[...]
    sum0 = out0[:256] + out2[1024:]
    sum1 = out0[256:] + out3[384:]
    sum2 = out1[:384] + out3[:384]
    sum3 = out1[384:] + out2[512:1024]
    sum4 = out2[:512]
    every = (0, 1, 2, 3)
    lower = wide < 64
    back2 = pltpu.roll(diagonal(sum2, 128, 128, (2, 3)), 64, 1)
    back3 = pltpu.roll(diagonal(sum3, 0, 128, every), 64, 1)
    back4 = pltpu.roll(diagonal(sum4, 0, 128, every), 64, 1)
    groups = (
        diagonal(sum0, 0, 64, every) + jnp.where(lower, back2, back3),
        diagonal(sum1, 0, 64, every) + jnp.where(lower, back3, back4),
        jnp.where(lower, diagonal(sum2, 0, 64, (0, 1)) + back4, diagonal(sum2, 192, 128, (2, 3))),
        diagonal(sum3, 64, 128, every),
        diagonal(sum4, 64, 128, every),
    )
    for n, group in enumerate(groups):
        staged.reshape(512, 128)[pl.ds(n, 64, stride=8), :] = group
    staged.reshape(512, 128)[pl.ds(5, 64, stride=8), :] = jnp.zeros((64, 128), F32)
    send2[...] = staged[:, :6, :].astype(BF16)

    def fourier_row(lat):
        row = jnp.where(lat < 32, lat, 95 - lat)
        return send2.at[row], recv2.at[band]

    def fourier_step(n, carry):
        plane = lax.rem(z + 4 + 3 * n, 8)
        for e in range(8):
            lat = plane * 8 + (rc ^ e)
            src, dst = fourier_row(lat)
            copy = pltpu.make_async_remote_copy(
                src_ref=src, dst_ref=dst, send_sem=ssem2, recv_sem=rsem2.at[half],
                device_id=(lat, lev), device_id_type=MESH,
            )
            if e:
                copy.start()
            else:
                pl.when(n != 4)(copy.start)
        return carry

    half = lax.div(band, 32)
    pl.semaphore_wait(told2, jnp.where(own_line, 7, 8))
    src, dst = fourier_row(band)
    pltpu.make_async_copy(src, dst, rsem2.at[half]).start()
    lax.fori_loop(0, 8, fourier_step, 0)
    chunk16 = lax.shift_right_logical(iota((16, 128), 1), 5)
    for part in range(2):
        arrived = recv2.at[pl.ds(32 * part, 32)]
        pltpu.make_async_copy(arrived, arrived, rsem2.at[part]).wait()
        staged[32 * part : 32 * part + 32, :6, :] = recv2[32 * part : 32 * part + 32].astype(F32)

        def received(n):
            rows = pl.ds(256 * part + n, 32, stride=8)
            return staged.reshape(512, 128)[rows, :]

        four = jnp.concatenate([received(n) for n in range(4)], axis=0).T
        last = jnp.concatenate([received(4)] * 4, axis=0).T

        def coefficients(c):
            tiles = [four[32 * n + 16 * c : 32 * n + 16 * c + 16] for n in range(4)]
            mixed = last[16 * c : 16 * c + 16]
            for n in range(1, 4):
                mixed = jnp.where(chunk16 == n, last[32 * n + 16 * c : 32 * n + 16 * c + 16], mixed)
            return tiles + [mixed]

        reals, imags = coefficients(0), coefficients(1)

        def twist(start, count):
            for tile in range(5):
                cols = slice((5 * part + tile) * 128, (5 * part + tile) * 128 + 128)
                real_cols = slice((10 * part + tile) * 128, (10 * part + tile) * 128 + 128)
                imag_cols = slice((10 * part + tile + 5) * 128, (10 * part + tile + 5) * 128 + 128)
                cosines, sines = cos_t[pl.ds(start, 8), cols], sin_t[pl.ds(start, 8), cols]
                real, imag = reals[tile], imags[tile]
                for n in range(count):
                    at = pl.ds(pl.multiple_of((start + n) * 16, 16), 16)
                    cosine, sine = cosines[n : n + 1], sines[n : n + 1]
                    tw[at, real_cols] = (real * cosine - imag * sine).astype(BF16)
                    tw[at, imag_cols] = (real * sine + imag * cosine).astype(BF16)

        def twist_step(n, carry):
            twist(pl.multiple_of(n * 8, 8), 8)
            return carry

        lax.fori_loop(0, 5, twist_step, 0)
        twist(40, 1)
        sums = dot_nn(tw[:, 1280 * part : 1280 * part + 1280], basis[1280 * part : 1280 * part + 1280, :])
        if part == 0:
            total_ref[...] = sums
        else:
            total = sums

    column = iota((16, 256), 1) & 127
    for b in range(BLOCKS):
        inside = (column + 128 * b).astype(F32) < row_len
        blocks[16 * b : 16 * b + 16, :] = jnp.where(inside, total[16 * b : 16 * b + 16] + total_ref[16 * b : 16 * b + 16, :], 0.0)

    @pl.when(own_line)
    def _():
        sent = send1.at[pl.ds(0, 63)]
        pltpu.make_async_copy(sent, sent, ssem1).wait()

    @pl.when(jnp.logical_not(own_line))
    def _():
        pltpu.make_async_copy(send1, send1, ssem1).wait()

    gone = send2.at[pl.ds(0, 63)]
    pltpu.make_async_copy(gone, gone, ssem2).wait()


def lay_out(blocks, out_f, out_s):
    for b in range(BLOCKS):
        width = min(128, LONMAX - 128 * b)
        for out, at in ((out_f, 0), (out_s, 128)):
            out[0, :, 128 * b : 128 * b + width] = blocks[16 * b : 16 * b + 16, at : at + width]


def shards(control, vertical_root, legendre, wave_list, row_length):
    shape = jax.ShapeDtypeStruct((1, 16, LONMAX), F32)
    vmem, hbm = pl.BlockSpec(memory_space=pltpu.VMEM), pl.BlockSpec(memory_space=pl.ANY)
    blocks = pl.pallas_call(
        kernel,
        out_shape=jax.ShapeDtypeStruct((16 * BLOCKS, 256), F32),
        in_specs=[hbm] * 5,
        out_specs=vmem,
        scratch_shapes=[
            pltpu.VMEM((20, 320, 128), BF16),
            pltpu.VMEM((20, 128, 128), BF16),
            pltpu.SMEM((1280,), jnp.int32),
            pltpu.VMEM((640, 1280), BF16),
            pltpu.SMEM((32,), jnp.int32),
            pltpu.VMEM((32 * 320, 128), F32),
            pltpu.VMEM((64, 54, 128), BF16),
            pltpu.VMEM((64, 54, 128), BF16),
            pltpu.VMEM((512, 1024), BF16),
            pltpu.VMEM((896, 1024), BF16),
            pltpu.VMEM((1280, 1024), BF16),
            pltpu.VMEM((640, 1024), BF16),
            pltpu.VMEM((64, 8, 128), F32),
            pltpu.VMEM((64, 6, 128), BF16),
            pltpu.VMEM((64, 6, 128), BF16),
            pltpu.VMEM((48, 1280), F32),
            pltpu.VMEM((48, 1280), F32),
            pltpu.VMEM((2560, 256), BF16),
            pltpu.VMEM((656, 2560), BF16),
            pltpu.VMEM((512, 128), F32),
            pltpu.VMEM((896, 128), F32),
            pltpu.VMEM((1280, 128), F32),
            pltpu.VMEM((640, 128), F32),
            pltpu.VMEM((656, 256), F32),
            pltpu.SemaphoreType.DMA((3,)),
            pltpu.SemaphoreType.DMA((4,)),
            pltpu.SemaphoreType.DMA((4,)),
            pltpu.SemaphoreType.DMA,
            pltpu.SemaphoreType.DMA((8,)),
            pltpu.SemaphoreType.DMA,
            pltpu.SemaphoreType.DMA((2,)),
            pltpu.SemaphoreType.REGULAR,
            pltpu.SemaphoreType.REGULAR,
        ],
        compiler_params=pltpu.CompilerParams(
            collective_id=0, has_side_effects=True, vmem_limit_bytes=56 * 2**20
        ),
    )(
        control.reshape(20, 320, 128),
        vertical_root,
        legendre.reshape(640, 1280),
        wave_list,
        row_length,
    )
    return pl.pallas_call(
        lay_out, out_shape=(shape, shape), in_specs=[vmem], out_specs=(vmem, vmem)
    )(blocks)


def solution(mesh):
    placed = (P("band", "lev", None, None), P("band", None, None), P("band", None, None), P(), P())
    return jax.shard_map(
        shards,
        mesh=mesh,
        in_specs=placed,
        out_specs=(P("band", "lev", None), P("band", "lev", None)),
        check_vma=False,
    )
```
